256 devices in a mesh: fsdp: 16 (over x_lo, y, core), seq: 16 (over x_hi, z).
Axes of the slice: x: 4 (x_hi: 2, x_lo: 2; x = x_hi * 2 + x_lo), y: 4, z: 8, core: 2. Of those that a mesh axis runs over, the one named last changes fastest.
Arguments:
- attn_inputs: bfloat16 [16, 2048, 3, 2048], P('fsdp', 'seq'), may hold values from -32 to 32
- out_weight: bfloat16 [2048, 3072], P('fsdp'), may hold values from -0.125 to 0.125
- skew_params: float32 [96, 128, 128], P('fsdp'), may hold values from -0.3 to 0.3
- piece_orders: int32 [4, 96], replicated, may hold values from 0 to 95, each once within a row
- cotangent: bfloat16 [16, 2048, 3072], P('fsdp', 'seq'), may hold values from -6 to 6
Outputs:
- block_output: bfloat16 [16, 2048, 3072], P('fsdp', 'seq')
- grad_inputs: bfloat16 [16, 2048, 3, 2048], P('fsdp', 'seq')
- grad_skew: float32 [96, 128, 128], P('fsdp')
The draws below stay inside these ranges and needn't reach their ends.
Inputs may be any that keep to these rules, and one draw needn't show every extreme that they name: `piece_orders`: each row lists every piece number from 0 to 95 exactly once.
All inputs are finite; a program needn't handle non-finite values.
Results may differ from the reference program's by a relative error of at most 0.03.
Values may be sent and summed in bfloat16 or wider, within the bound.
No kernel may reach another device: no remote copies, remote signals or barrier semaphores. Data moves between devices by JAX's collectives and lax.ppermute only.
A program may use at most 128 MiB of HBM per device.

```python
import math
import jax
import jax.numpy as jnp
from jax import lax

D = 3072
HEADS = 16
HD = 128
BS = 128
FACTORS = 4
LENGTH = 2048
SEQS = 16
HW = 2048
PIECES = 96
BLOCKS = 96


def draw_attn_inputs(key, part):
    key = jax.random.fold_in(key, 17)
    base_key = jax.random.fold_in(key, 0)
    shape = (SEQS, LENGTH, 3, HEADS * HD)
    values = jnp.clip(jax.random.normal(base_key, shape, jnp.float32), -6.0, 6.0)
    return values.astype(jnp.bfloat16)


def with_spikes(array, rng, source, target, blocks, factor):
    def block_of(axis_at):
        return (jnp.arange(array.shape[axis_at]) // (array.shape[axis_at] // blocks)).reshape((-1,) + (1,) * (array.ndim - 1 - axis_at))

    first = jax.random.permutation(rng, blocks)[block_of(target)]
    other_side = (block_of(target) + blocks // 2) % blocks
    return jnp.where((block_of(source) == first) | (block_of(source) == other_side), factor * array, array)


def levels(stream_key, shape, cuts, least, high):
    factor_of, own = 1.0, jax.random.fold_in(stream_key, 6)
    for position, parts in cuts:
        draws = jnp.exp(jax.random.uniform(jax.random.fold_in(own, position), (parts,), jnp.float32, least / len(cuts), high / len(cuts)))
        factor_of = factor_of * jnp.repeat(draws, shape[position] // parts).reshape([-1 if axis == position else 1 for axis in range(len(shape))])
    return factor_of


def normal_values(rng, extent, deviation, reach, cuts=(), kind=jnp.bfloat16):
    level = levels(rng, extent, cuts, -0.22, 0.18) if cuts else 1.0
    entries = jax.random.normal(rng, extent, jnp.float32) * deviation * level
    return jnp.minimum(jnp.maximum(entries, -reach), reach).astype(kind)


def noise_with(key, extent, spread, limit, shards, heavy, held_as=jnp.bfloat16):
    entries = spread * jax.random.normal(key, extent, jnp.float32)
    if shards:
        entries = entries * levels(key, extent, shards, -0.22, 0.18)
    return jnp.clip(with_spikes(entries, jax.random.fold_in(key, 3), *heavy), -limit, limit).astype(held_as)


def setup_inputs(seed: int = 0) -> dict:
    seeds = jax.random.split(jax.random.key(seed), 6)
    return {
        "attn_inputs": draw_attn_inputs(jax.random.fold_in(seeds[5], 71), 0),
        "out_weight": normal_values(seeds[1], (HW, D), HW ** -0.5, 0.125, ((0, 16),)),
        "skew_params": normal_values(seeds[2], (BLOCKS, BS, BS), 0.05, 0.3, ((0, 16),), jnp.float32),
        "piece_orders": jax.vmap(lambda own: jax.random.permutation(own, PIECES))(jax.random.split(seeds[3], FACTORS)).reshape((FACTORS, PIECES)).astype(jnp.int32),
        "cotangent": noise_with(seeds[4], (SEQS, LENGTH, D), 1.0, 6.0, ((0, 16), (1, 16)), (0, 2, 16, 2.0)),
    }


def cayley(skew_params):
    skewed = skew_params - jnp.swapaxes(skew_params, -1, -2)
    identity = jnp.eye(skew_params.shape[-1], dtype=skew_params.dtype)
    minus_part = identity - skewed
    gram_matrix = identity + jnp.matmul(jnp.swapaxes(skewed, -1, -2), skewed, precision=lax.Precision.HIGHEST)
    factor_low = jnp.linalg.cholesky(gram_matrix)
    halfway = lax.linalg.triangular_solve(factor_low, minus_part, left_side=True, lower=True)
    solved = lax.linalg.triangular_solve(factor_low, halfway, left_side=True, lower=True, transpose_a=True)
    return jnp.matmul(minus_part, solved, precision=lax.Precision.HIGHEST)

def reorder(matrix, ordering):
    row_count = matrix.shape[0]
    return jnp.take(matrix.reshape(row_count, ordering.shape[0], -1), ordering, axis=1).reshape(row_count, -1)

def inverse_order(ordering):
    return jnp.zeros_like(ordering).at[ordering].set(jnp.arange(ordering.shape[0], dtype=jnp.int32))

def head_probs(queries, key_rows):
    scores = jnp.dot(queries.astype(jnp.float32), key_rows.T.astype(jnp.float32), preferred_element_type=jnp.float32) * (1.0 / math.sqrt(HD))
    shifted = jnp.exp(scores - lax.optimization_barrier(jnp.max(scores, axis=-1, keepdims=True)))
    return shifted / lax.optimization_barrier(jnp.sum(shifted, axis=-1, keepdims=True))

def reference(attn_inputs, out_weight, skew_params, piece_orders, cotangent):
    blocks_per = D // BS
    total_rows = SEQS * LENGTH
    rotations = cayley(skew_params).astype(jnp.bfloat16).reshape(FACTORS, blocks_per, BS, BS)
    per_head = attn_inputs.reshape(SEQS, LENGTH, 3, HEADS, HD).transpose(0, 3, 2, 1, 4)

    def clip_forward(clip_data):

        def one_head(triple):
            softmaxed = head_probs(triple[0], triple[1])
            return jnp.dot(softmaxed.astype(jnp.bfloat16).astype(jnp.float32), triple[2].astype(jnp.float32), preferred_element_type=jnp.float32).astype(jnp.bfloat16)
        return lax.map(one_head, clip_data)
    attended = lax.map(clip_forward, per_head)
    attended_rows = attended.transpose(0, 2, 1, 3).reshape(total_rows, HW)
    projected = jnp.dot(attended_rows.astype(jnp.float32), out_weight.astype(jnp.float32), preferred_element_type=jnp.float32).astype(jnp.bfloat16)
    current = projected
    saved_rows = []
    for factor in range(FACTORS):
        ordering = piece_orders[factor]
        moved_rows = reorder(current, ordering).reshape(total_rows, blocks_per, BS)
        saved_rows.append(moved_rows)
        mixed_rows = jnp.einsum('tjb,jbc->tjc', moved_rows.astype(jnp.float32), rotations[factor].astype(jnp.float32))
        current = reorder(mixed_rows.reshape(total_rows, D), inverse_order(ordering)).astype(jnp.bfloat16)
    block_output = current.reshape(SEQS, LENGTH, D)
    upstream = cotangent.reshape(total_rows, D)
    pieces_grad = [None] * FACTORS
    for factor in reversed(range(FACTORS)):
        ordering = piece_orders[factor]
        moved_grad = reorder(upstream, ordering).reshape(total_rows, blocks_per, BS)
        pieces_grad[factor] = jnp.einsum('tjb,tjc->jbc', saved_rows[factor].astype(jnp.float32), moved_grad.astype(jnp.float32))
        back_mixed = jnp.einsum('tjc,jbc->tjb', moved_grad.astype(jnp.float32), rotations[factor].astype(jnp.float32))
        upstream = reorder(back_mixed.reshape(total_rows, D), inverse_order(ordering)).astype(jnp.bfloat16)
    rot_grad = jnp.stack(pieces_grad).reshape(FACTORS * blocks_per, BS, BS)
    grad_attended = jnp.dot(upstream.astype(jnp.float32), out_weight.T.astype(jnp.float32), preferred_element_type=jnp.float32).astype(jnp.bfloat16)
    grad_attended = grad_attended.reshape(SEQS, LENGTH, HEADS, HD).transpose(0, 2, 1, 3)

    def clip_backward(packed):
        clip_data, clip_douts = packed

        def one_head(pair_items):
            triple, head_dout = pair_items
            rounded = head_probs(triple[0], triple[1]).astype(jnp.bfloat16)
            widened = rounded.astype(jnp.float32)
            dprobs = jnp.dot(head_dout.astype(jnp.float32), triple[2].T.astype(jnp.float32), preferred_element_type=jnp.float32)
            centre = lax.optimization_barrier(jnp.sum(widened * dprobs, axis=-1, keepdims=True))
            dscores = (widened * (dprobs - centre) * (1.0 / math.sqrt(HD))).astype(jnp.bfloat16)
            grad_q = jnp.dot(dscores.astype(jnp.float32), triple[1].astype(jnp.float32), preferred_element_type=jnp.float32).astype(jnp.bfloat16)
            grad_k = jnp.dot(dscores.T.astype(jnp.float32), triple[0].astype(jnp.float32), preferred_element_type=jnp.float32).astype(jnp.bfloat16)
            grad_v = jnp.dot(rounded.T.astype(jnp.float32), head_dout.astype(jnp.float32), preferred_element_type=jnp.float32).astype(jnp.bfloat16)
            return jnp.stack([grad_q, grad_k, grad_v])
        return lax.map(one_head, (clip_data, clip_douts))
    head_grads = lax.map(clip_backward, (per_head, grad_attended))
    grad_inputs = head_grads.transpose(0, 3, 2, 1, 4).reshape(SEQS, LENGTH, 3, HW)
    unused, pullback = jax.vjp(cayley, skew_params)
    grad_skew = pullback(rot_grad * (1.0 / math.sqrt(SEQS * LENGTH)))[0]
    return (block_output, grad_inputs, grad_skew)
```

```python
import functools
import math

import jax
import jax.numpy as jnp
from jax import lax
from jax.experimental import pallas as pl
from jax.experimental.pallas import tpu as pltpu
from jax.sharding import Mesh, PartitionSpec as P

HEADS = 16
HD = 128
BS = 128
FACTORS = 4
PIECE = 32
PER = BS // PIECE
BF = jnp.bfloat16
F32 = jnp.float32
HIGH = lax.Precision.HIGHEST
ROWS = ("xl", "y", "c")
SEQ = ("xh", "z")
QB = 256
LOG2E = 1.4426950408889634
MIB = 1024 * 1024


def params(limit, semantics=None):
    return pltpu.CompilerParams(vmem_limit_bytes=limit * MIB, dimension_semantics=semantics)


def inverse_kernel(skew_ref, inv_ref, rot_ref):
    count, size, _ = skew_ref.shape
    row = lax.broadcasted_iota(jnp.int32, (size, size), 0)
    col = lax.broadcasted_iota(jnp.int32, (size, size), 1)
    eye = (row == col).astype(F32)
    row8 = lax.broadcasted_iota(jnp.int32, (8, size), 0)
    col8 = lax.broadcasted_iota(jnp.int32, (8, size), 1)
    eye8 = (row8 == col8).astype(F32)
    rowp = lax.broadcasted_iota(jnp.int32, (size, 8), 0)
    colp = lax.broadcasted_iota(jnp.int32, (size, 8), 1)
    for b in range(count):
        params_b = skew_ref[b]
        inv_ref[b] = eye + params_b - params_b.T

    def step(g, carry):
        first = pl.multiple_of(g * 8, 8)
        panels = [inv_ref[b, pl.ds(first, 8), :] for b in range(count)]
        sides = [eye8] * count
        for j in range(8):
            pick = (lax.broadcasted_iota(jnp.int32, (8, 1), 0) == j).astype(F32)
            for b in range(count):
                panel, side = panels[b], sides[b]
                column = panel[:, j : j + 1]
                scale = 1.0 / panel[j : j + 1, j : j + 1]
                left = (column - pick) * scale
                panels[b] = panel - left * panel[j : j + 1, :]
                sides[b] = side - left * side[j : j + 1, :]
        selector = (rowp - first == colp).astype(F32)
        for b in range(count):
            whole = inv_ref[b]
            update = jnp.dot(
                whole[:, :8] - selector,
                panels[b] + sides[b],
                precision=HIGH,
                preferred_element_type=F32,
            )
            inv_ref[b] = pltpu.roll(whole - update, size - 8, 1)
        return carry

    lax.fori_loop(0, size // 8, step, 0)
    for b in range(count):
        rot_ref[b] = (2.0 * inv_ref[b] - eye).astype(BF)


def cayley(skew):
    return pl.pallas_call(
        inverse_kernel,
        out_shape=(
            jax.ShapeDtypeStruct(skew.shape, F32),
            jax.ShapeDtypeStruct(skew.shape, BF),
        ),
        compiler_params=params(32),
        name="cayley",
    )(skew)


def pullback_kernel(scaling, inv_ref, grad_ref, out_ref):
    for b in range(inv_ref.shape[0]):
        flipped = inv_ref[b].T
        grad = grad_ref[b].astype(F32) * (-2.0 * scaling)
        inner = jnp.dot(flipped, grad, precision=HIGH, preferred_element_type=F32)
        grad_s = jnp.dot(inner, flipped, precision=HIGH, preferred_element_type=F32)
        out_ref[b] = grad_s - grad_s.T


def cayley_pullback(inverse, grad, scaling):
    return pl.pallas_call(
        functools.partial(pullback_kernel, scaling),
        out_shape=jax.ShapeDtypeStruct(inverse.shape, F32),
        compiler_params=params(32),
        name="cayley_pullback",
    )(inverse, grad)


def attend_kernel(q_ref, k_ref, v_ref, att_ref, wide_ref, exps_ref, sums_ref, vt_ref):
    @pl.when(pl.program_id(0) == 0)
    def _():
        vt_ref[...] = v_ref[...].reshape(-1, HD).T

    queries = q_ref[...].reshape(QB, HD)
    keys = k_ref[...].reshape(-1, HD)
    scores = lax.dot_general(keys, queries, (((1,), (1,)), ((), ())), preferred_element_type=F32)
    factor = LOG2E / math.sqrt(HD)
    top = jnp.max(scores, axis=0, keepdims=True)
    exps = jnp.exp2((scores - top) * factor)
    total = jnp.sum(exps, axis=0, keepdims=True)
    low = exps.astype(BF)
    exps_ref[0] = low
    wide = jnp.dot(vt_ref[...], low, preferred_element_type=F32) / total
    wide_ref[0] = wide
    sums_ref[0] = 1.0 / total
    att_ref[...] = wide.T.astype(BF).reshape(att_ref.shape)


def attend(spread):
    groups, _, tok, _ = spread.shape
    length = groups * tok
    per = QB // tok
    steps = length // QB
    return pl.pallas_call(
        attend_kernel,
        grid=(steps,),
        in_specs=[
            pl.BlockSpec((per, 1, tok, HD), lambda i: (i, 0, 0, 0)),
            pl.BlockSpec((groups, 1, tok, HD), lambda i: (0, 1, 0, 0)),
            pl.BlockSpec((groups, 1, tok, HD), lambda i: (0, 2, 0, 0)),
        ],
        out_specs=[
            pl.BlockSpec((per, tok, HD), lambda i: (i, 0, 0)),
            pl.BlockSpec((1, HD, QB), lambda i: (i, 0, 0)),
            pl.BlockSpec((1, length, QB), lambda i: (i, 0, 0)),
            pl.BlockSpec((1, 1, QB), lambda i: (i, 0, 0)),
        ],
        out_shape=[
            jax.ShapeDtypeStruct((groups, tok, HD), BF),
            jax.ShapeDtypeStruct((steps, HD, QB), F32),
            jax.ShapeDtypeStruct((steps, length, QB), BF),
            jax.ShapeDtypeStruct((steps, 1, QB), F32),
        ],
        scratch_shapes=[pltpu.VMEM((HD, length), BF)],
        compiler_params=params(58, ("arbitrary",)),
        cost_estimate=pl.CostEstimate(
            flops=4 * length * length * HD, bytes_accessed=2 * length * length, transcendentals=length * length
        ),
        name="attend",
    )(spread, spread, spread)


def attend_back_kernel(
    q_ref, k_ref, v_ref, dout_ref, wide_ref, exps_ref, sums_ref, out_ref, kt_ref, dk_ref, dv_ref
):
    step = pl.program_id(0)
    groups, _, tok, _ = k_ref.shape
    per = QB // tok

    @pl.when(step == 0)
    def _():
        kt_ref[...] = k_ref[...].reshape(-1, HD).T
        dk_ref[...] = jnp.zeros_like(dk_ref)
        dv_ref[...] = jnp.zeros_like(dv_ref)

    queries = q_ref[...].reshape(QB, HD)
    values = v_ref[...].reshape(-1, HD)
    dout = jnp.concatenate([dout_ref[p] for p in range(per)], axis=1)
    inv_sum = sums_ref[0]
    wide_dout = dout.astype(F32)
    low = exps_ref[0]
    dv_ref[...] += lax.dot_general(
        low, (wide_dout * inv_sum).astype(BF), (((1,), (1,)), ((), ())), preferred_element_type=F32
    )
    centre = jnp.sum(wide_dout * wide_ref[0], axis=0, keepdims=True)
    dprobs = jnp.dot(values, dout, preferred_element_type=F32)
    dscores = (low.astype(F32) * ((dprobs - centre) * (inv_sum * (1.0 / math.sqrt(HD))))).astype(BF)
    dk_ref[...] += jnp.dot(dscores, queries, preferred_element_type=F32)
    dq = jnp.dot(kt_ref[...], dscores, preferred_element_type=F32)
    out_ref[pl.ds(step * per, per), 0] = dq.T.astype(BF).reshape(per, tok, HD)

    @pl.when(step == pl.num_programs(0) - 1)
    def _():
        out_ref[:, 1] = dk_ref[...].astype(BF).reshape(groups, tok, HD)
        out_ref[:, 2] = dv_ref[...].astype(BF).reshape(groups, tok, HD)


def attend_back(spread, dout, wide, exps, sums):
    groups, _, tok, _ = spread.shape
    length = groups * tok
    per = QB // tok
    steps = length // QB
    return pl.pallas_call(
        attend_back_kernel,
        grid=(steps,),
        in_specs=[
            pl.BlockSpec((per, 1, tok, HD), lambda i: (i, 0, 0, 0)),
            pl.BlockSpec((groups, 1, tok, HD), lambda i: (0, 1, 0, 0)),
            pl.BlockSpec((groups, 1, tok, HD), lambda i: (0, 2, 0, 0)),
            pl.BlockSpec((per, HD, tok), lambda i: (i, 0, 0)),
            pl.BlockSpec((1, HD, QB), lambda i: (i, 0, 0)),
            pl.BlockSpec((1, length, QB), lambda i: (i, 0, 0)),
            pl.BlockSpec((1, 1, QB), lambda i: (i, 0, 0)),
        ],
        out_specs=pl.BlockSpec((groups, 3, tok, HD), lambda i: (0, 0, 0, 0)),
        out_shape=jax.ShapeDtypeStruct((groups, 3, tok, HD), BF),
        scratch_shapes=[
            pltpu.VMEM((HD, length), BF),
            pltpu.VMEM((length, HD), F32),
            pltpu.VMEM((length, HD), F32),
        ],
        compiler_params=params(58, ("arbitrary",)),
        cost_estimate=pl.CostEstimate(
            flops=8 * length * length * HD, bytes_accessed=2 * length * length, transcendentals=0
        ),
        name="attend_back",
    )(spread, spread, spread, dout, wide, exps, sums)


def gather_block(order_ref, factor, j, source_ref):
    pieces = []
    for p in range(PER):
        at = pl.multiple_of(order_ref[factor, j * PER + p] * PIECE, PIECE)
        pieces.append(source_ref[pl.ds(at, PIECE), :])
    return jnp.concatenate(pieces, axis=0)


def scatter_block(order_ref, factor, j, block, target_ref):
    for p in range(PER):
        at = pl.multiple_of(order_ref[factor, j * PER + p] * PIECE, PIECE)
        target_ref[pl.ds(at, PIECE), :] = block[p * PIECE : (p + 1) * PIECE, :]


def down_kernel(order_ref, home_ref, cot_ref, near_ref, far_ref, moved_ref, up_ref, flip_ref, rot_ref, a_ref, b_ref):
    blocks = cot_ref.shape[1] // BS
    half = near_ref.shape[0]

    def place(i, carry):
        for base, source in ((0, near_ref), (half, far_ref)):
            rot = source[i]
            at = home_ref[base + i]
            rot_ref[at] = rot
            flip_ref[at] = rot.T
        return carry

    lax.fori_loop(0, half, place, 0, unroll=4)
    for j in range(blocks):
        a_ref[j * BS : (j + 1) * BS, :] = cot_ref[:, j * BS : (j + 1) * BS].T
    source, target = a_ref, b_ref
    for factor in reversed(range(FACTORS)):
        if factor == 0:
            target = up_ref

        def body(j, carry, factor=factor, source=source, target=target):
            block = gather_block(order_ref, factor, j, source)
            moved_ref[factor, pl.ds(pl.multiple_of(j * BS, BS), BS), :] = block
            back = jnp.dot(
                rot_ref[factor * blocks + j], block, preferred_element_type=F32
            ).astype(BF)
            scatter_block(order_ref, factor, j, back, target)
            return carry

        lax.fori_loop(0, blocks, body, 0, unroll=4)
        source, target = target, source


def down(orders, home, cotangent, near, far):
    tok, width = cotangent.shape
    total = 2 * near.shape[0]
    smem = pl.BlockSpec(memory_space=pltpu.SMEM)
    vmem = pl.BlockSpec(memory_space=pltpu.VMEM)
    return pl.pallas_call(
        down_kernel,
        in_specs=[smem, smem, vmem, vmem, vmem],
        out_specs=[vmem, vmem, vmem],
        out_shape=[
            jax.ShapeDtypeStruct((FACTORS, width, tok), BF),
            jax.ShapeDtypeStruct((width, tok), BF),
            jax.ShapeDtypeStruct((total, BS, BS), BF),
        ],
        scratch_shapes=[
            pltpu.VMEM((total, BS, BS), BF),
            pltpu.VMEM((width, tok), BF),
            pltpu.VMEM((width, tok), BF),
        ],
        compiler_params=params(40),
        cost_estimate=pl.CostEstimate(flops=10**9, bytes_accessed=10**7, transcendentals=0),
        name="butterfly_down",
    )(orders, home, cotangent, near, far)


def up_kernel(order_ref, self_ref, proj_ref, flip_ref, moved_ref, out_ref, mine_ref, other_ref, a_ref, b_ref):
    blocks = proj_ref.shape[1] // BS
    owned = mine_ref.shape[1]
    xl, y, core = self_ref[0], self_ref[1], self_ref[2]
    for j in range(blocks):
        a_ref[j * BS : (j + 1) * BS, :] = proj_ref[:, j * BS : (j + 1) * BS].T
    source, target = a_ref, b_ref
    for factor in range(FACTORS):
        for half, grad_ref in ((core, mine_ref), (1 - core, other_ref)):

            def body(i, carry, factor=factor, source=source, target=target, half=half, grad_ref=grad_ref):
                pair, inside = i // owned, i % owned
                j = (2 * pair + half) * owned + inside
                at = factor * blocks + j
                block = gather_block(order_ref, factor, j, source)
                mixed = jnp.dot(flip_ref[at], block, preferred_element_type=F32).astype(BF)
                scatter_block(order_ref, factor, j, mixed, target)
                moved = moved_ref[factor, pl.ds(pl.multiple_of(j * BS, BS), BS), :]
                owner = factor * (blocks // (2 * owned)) + pair
                slot = ((owner // 4) ^ xl) * 4 + ((owner % 4 + 4 - y) % 4)
                grad_ref[slot, inside] = lax.dot_general(
                    block, moved, (((1,), (1,)), ((), ())), preferred_element_type=F32
                ).astype(BF)
                return carry

            lax.fori_loop(0, blocks // 2, body, 0, unroll=4)
        source, target = target, source
    for j in range(blocks):
        out_ref[:, j * BS : (j + 1) * BS] = source[j * BS : (j + 1) * BS, :].T


def up(orders, position, projected, flipped, moved):
    tok, width = projected.shape
    smem = pl.BlockSpec(memory_space=pltpu.SMEM)
    vmem = pl.BlockSpec(memory_space=pltpu.VMEM)
    owned = flipped.shape[0] // 16
    half = jax.ShapeDtypeStruct((8, owned, BS, BS), BF)
    return pl.pallas_call(
        up_kernel,
        in_specs=[smem, smem, vmem, vmem, vmem],
        out_specs=[vmem, vmem, vmem],
        out_shape=[jax.ShapeDtypeStruct((tok, width), BF), half, half],
        scratch_shapes=[pltpu.VMEM((width, tok), BF), pltpu.VMEM((width, tok), BF)],
        compiler_params=params(40),
        cost_estimate=pl.CostEstimate(flops=10**9, bytes_accessed=10**7, transcendentals=0),
        name="butterfly_up",
    )(orders, position, projected, flipped, moved)


def products_kernel(weight_ref, up_ref, att_ref, back_ref, proj_ref, acc_ref):
    step = pl.program_id(0)
    weight = weight_ref[...]
    back_ref[...] = jnp.dot(weight, up_ref[...], preferred_element_type=F32).astype(BF)
    att = jnp.concatenate([att_ref[p] for p in range(att_ref.shape[0])], axis=1)
    term = jnp.dot(att, weight, preferred_element_type=F32)

    @pl.when(step == 0)
    def _():
        acc_ref[...] = term

    @pl.when(step > 0)
    def _():
        acc_ref[...] += term

    @pl.when(step == pl.num_programs(0) - 1)
    def _():
        proj_ref[...] = acc_ref[...].astype(BF)


def products(weight, upstream, att):
    rows, width = weight.shape
    tok = upstream.shape[1]
    tile = 256
    return pl.pallas_call(
        products_kernel,
        grid=(rows // tile,),
        in_specs=[
            pl.BlockSpec((tile, width), lambda i: (i, 0)),
            pl.BlockSpec((width, tok), lambda i: (0, 0)),
            pl.BlockSpec((tile // HD, tok, HD), lambda i: (i, 0, 0)),
        ],
        out_specs=[
            pl.BlockSpec((tile, tok), lambda i: (i, 0)),
            pl.BlockSpec((tok, width), lambda i: (0, 0)),
        ],
        out_shape=[
            jax.ShapeDtypeStruct((rows, tok), BF),
            jax.ShapeDtypeStruct((tok, width), BF),
        ],
        scratch_shapes=[pltpu.VMEM((tok, width), F32)],
        compiler_params=params(58, ("arbitrary",)),
        cost_estimate=pl.CostEstimate(
            flops=4 * rows * width * tok, bytes_accessed=2 * rows * width, transcendentals=0
        ),
        name="products",
    )(weight, upstream, att)


def swap(x, axis):
    return lax.ppermute(x, axis, [(0, 1), (1, 0)])


def shift(x, axis, by):
    n = lax.axis_size(axis)
    return lax.ppermute(x, axis, [(i, (i + by) % n) for i in range(n)])


def turn(x, by):
    order = [(x_hi * 2 + x_lo) for x_lo in range(2) for x_hi in range(2)]
    at = {x: i for i, x in enumerate(order)}
    return lax.ppermute(x, ("xl", "xh"), [(at[i], at[(i + by) % 4]) for i in range(4)])


def cross(x):
    half = x.shape[0] // 2
    return jnp.concatenate([turn(x[:half], 1), turn(x[half:], 3)], axis=0)


def partner(x, axis, bit):
    return lax.ppermute(x, axis, [(i, i ^ bit) for i in range(lax.axis_size(axis))])


def add(*terms):
    return sum(t.astype(F32) for t in terms).astype(BF)


def after(x, *others):
    return lax.optimization_barrier((x,) + others)[0]


def gather_column(own):
    return jnp.concatenate([own, shift(own, "y", 1), shift(own, "y", 3), shift(own, "y", 2)], axis=0)


def gather_blocks(column, earlier):
    count = column.shape[0] // 4
    near = jnp.concatenate([column, after(cross(column), earlier)], axis=0)
    far = swap(near, "c")
    at = jnp.arange(16 * count, dtype=jnp.int32)
    slot, inside = at // count, at % count
    back = jnp.array([0, 1, 3, 2], jnp.int32)[slot % 4]
    y = (lax.axis_index("y") - back) % 4
    xl = lax.axis_index("xl") ^ ((slot // 4) % 2)
    c = lax.axis_index("c") ^ (slot // 8)
    return near, far, ((xl * 4 + y) * 2 + c) * count + inside


def local(attn_inputs, out_weight, skew_params, piece_orders, cotangent):
    tok = attn_inputs.shape[1]
    width = out_weight.shape[1]
    seqs = 16
    position = jnp.stack([lax.axis_index(a) for a in ROWS]).astype(jnp.int32)
    weight = lax.all_gather(out_weight, ROWS, axis=0, tiled=True)
    rows = attn_inputs[0].reshape(tok, 3, seqs, HD).transpose(2, 1, 0, 3)
    spread = lax.all_to_all(rows, SEQ, split_axis=0, concat_axis=0, tiled=True)
    inverse, rot_own = cayley(after(skew_params, rows))
    column = gather_column(rot_own)
    spread, column = lax.optimization_barrier((spread, column))
    att, wide, exps, sums = attend(spread)
    att_own = lax.all_to_all(att, SEQ, split_axis=0, concat_axis=0, tiled=True)
    near, far, home = gather_blocks(column, att_own)
    moved_grad, upstream, flipped = down(piece_orders, home, cotangent[0], near, far)
    grad_att, projected = products(weight, upstream, att_own)
    dout = lax.all_to_all(
        grad_att.reshape(seqs, HD, tok), SEQ, split_axis=0, concat_axis=0, tiled=True
    )
    block_output, mine, other = up(piece_orders, position, projected, flipped, moved_grad)
    mine, other, dout = lax.optimization_barrier((mine, other, dout))
    from_core = swap(other, "c")
    send = add(mine[4:], from_core[4:])
    from_xl = cross(send)
    grads = attend_back(spread, after(dout, send), wide, exps, sums)
    from_xl, grads = lax.optimization_barrier((from_xl, grads))
    grads = lax.all_to_all(grads, SEQ, split_axis=0, concat_axis=0, tiled=True)
    grad_inputs = grads.transpose(2, 1, 0, 3).reshape(1, tok, 3, seqs * HD)
    share = add(mine[:4], from_core[:4], from_xl)
    owner_grad = add(share[0], *[shift(share[dy], "y", dy) for dy in (2, 1, 3)])
    for axis, bit in (("xh", 1), ("z", 1), ("z", 2), ("z", 4)):
        owner_grad = add(owner_grad, partner(owner_grad, axis, bit))
    total_tokens = 16 * tok * seqs
    grad_skew = cayley_pullback(inverse, owner_grad, 1.0 / math.sqrt(total_tokens))
    return block_output[None], grad_inputs, grad_skew


def solution(mesh):
    fine = Mesh(mesh.devices.reshape(2, 4, 2, 2, 8), ROWS + SEQ)
    in_specs = (
        P(ROWS, SEQ, None, None),
        P(ROWS, None),
        P(ROWS, None, None),
        P(),
        P(ROWS, SEQ, None),
    )
    out_specs = (P(ROWS, SEQ, None), P(ROWS, SEQ, None, None), P(ROWS, None, None))
    return jax.shard_map(local, mesh=fine, in_specs=in_specs, out_specs=out_specs, check_vma=False)
```

```python
import functools
import math

import jax
import jax.numpy as jnp
from jax import lax
from jax.experimental import pallas as pl
from jax.experimental.pallas import tpu as pltpu
from jax.sharding import Mesh, PartitionSpec as P

HEADS = 16
HD = 128
BS = 128
FACTORS = 4
PIECE = 32
PER = BS // PIECE
BF = jnp.bfloat16
F32 = jnp.float32
HIGH = lax.Precision.HIGHEST
ROWS = ("xl", "y", "c")
SEQ = ("xh", "z")
QB = 512
KB = 2048
PANEL = 32
LOG2E = 1.4426950408889634
MIB = 1024 * 1024


def params(limit, semantics=None):
    return pltpu.CompilerParams(vmem_limit_bytes=limit * MIB, dimension_semantics=semantics)


def inverse_kernel(skew_ref, inv_ref, rot_ref):
    count, size, _ = skew_ref.shape
    row = lax.broadcasted_iota(jnp.int32, (size, size), 0)
    col = lax.broadcasted_iota(jnp.int32, (size, size), 1)
    eye = (row == col).astype(F32)
    eye_panel = eye[:PANEL]
    rowp = lax.broadcasted_iota(jnp.int32, (size, PANEL), 0)
    colp = lax.broadcasted_iota(jnp.int32, (size, PANEL), 1)
    for b in range(count):
        params_b = skew_ref[b]
        inv_ref[b] = eye + params_b - params_b.T

    def step(g, carry):
        first = pl.multiple_of(g * PANEL, PANEL)
        panels = [inv_ref[b, pl.ds(first, PANEL), :] for b in range(count)]
        sides = [eye_panel] * count
        for j in range(PANEL):
            pick = (lax.broadcasted_iota(jnp.int32, (PANEL, 1), 0) == j).astype(F32)
            for b in range(count):
                panel, side = panels[b], sides[b]
                scale = 1.0 / panel[j : j + 1, j : j + 1]
                left = panel[:, j : j + 1] - pick
                panels[b] = panel - left * (panel[j : j + 1, :] * scale)
                sides[b] = side - left * (side[j : j + 1, :] * scale)
        selector = (rowp - first == colp).astype(F32)
        for b in range(count):
            whole = inv_ref[b]
            update = jnp.dot(
                whole[:, :PANEL] - selector,
                panels[b] + sides[b],
                precision=HIGH,
                preferred_element_type=F32,
            )
            inv_ref[b] = pltpu.roll(whole - update, size - PANEL, 1)
        return carry

    lax.fori_loop(0, size // PANEL, step, 0)
    for b in range(count):
        rot_ref[b] = (2.0 * inv_ref[b] - eye).astype(BF)


def cayley(skew):
    return pl.pallas_call(
        inverse_kernel,
        out_shape=(
            jax.ShapeDtypeStruct(skew.shape, F32),
            jax.ShapeDtypeStruct(skew.shape, BF),
        ),
        compiler_params=params(32),
        name="cayley",
    )(skew)


def pullback_kernel(scaling, inv_ref, grad_ref, out_ref):
    for b in range(inv_ref.shape[0]):
        flipped = inv_ref[b].T
        grad = grad_ref[b].astype(F32) * (-2.0 * scaling)
        inner = jnp.dot(flipped, grad, precision=HIGH, preferred_element_type=F32)
        grad_s = jnp.dot(inner, flipped, precision=HIGH, preferred_element_type=F32)
        out_ref[b] = grad_s - grad_s.T


def cayley_pullback(inverse, grad, scaling):
    return pl.pallas_call(
        functools.partial(pullback_kernel, scaling),
        out_shape=jax.ShapeDtypeStruct(inverse.shape, F32),
        compiler_params=params(32),
        name="cayley_pullback",
    )(inverse, grad)


def attend_kernel(q_ref, k_ref, v_ref, att_ref, wide_ref, exps_ref, sums_ref, vt_ref):
    @pl.when(pl.program_id(0) == 0)
    def _():
        vt_ref[...] = v_ref[...].reshape(-1, HD).T

    queries = q_ref[...].reshape(QB, HD)
    groups, _, tok, _ = k_ref.shape
    length = groups * tok
    per = KB // tok
    factor = LOG2E / math.sqrt(HD)
    scores = []
    for c in range(length // KB):
        keys = k_ref[c * per : (c + 1) * per].reshape(KB, HD)
        scores.append(
            lax.dot_general(keys, queries, (((1,), (1,)), ((), ())), preferred_element_type=F32)
        )
    top = functools.reduce(jnp.maximum, [jnp.max(s, axis=0, keepdims=True) for s in scores])
    total, wide = 0.0, 0.0
    for c, part in enumerate(scores):
        exps = jnp.exp2((part - top) * factor)
        total += jnp.sum(exps, axis=0, keepdims=True)
        low = exps.astype(BF)
        exps_ref[0, c * KB : (c + 1) * KB, :] = low
        wide += jnp.dot(vt_ref[:, c * KB : (c + 1) * KB], low, preferred_element_type=F32)
    wide = wide / total
    wide_ref[0] = wide
    sums_ref[0] = 1.0 / total
    att_ref[...] = wide.T.astype(BF).reshape(att_ref.shape)


def attend(spread):
    groups, _, tok, _ = spread.shape
    length = groups * tok
    per = QB // tok
    steps = length // QB
    return pl.pallas_call(
        attend_kernel,
        grid=(steps,),
        in_specs=[
            pl.BlockSpec((per, 1, tok, HD), lambda i: (i, 0, 0, 0)),
            pl.BlockSpec((groups, 1, tok, HD), lambda i: (0, 1, 0, 0)),
            pl.BlockSpec((groups, 1, tok, HD), lambda i: (0, 2, 0, 0)),
        ],
        out_specs=[
            pl.BlockSpec((per, tok, HD), lambda i: (i, 0, 0)),
            pl.BlockSpec((1, HD, QB), lambda i: (i, 0, 0)),
            pl.BlockSpec((1, length, QB), lambda i: (i, 0, 0)),
            pl.BlockSpec((1, 1, QB), lambda i: (i, 0, 0)),
        ],
        out_shape=[
            jax.ShapeDtypeStruct((groups, tok, HD), BF),
            jax.ShapeDtypeStruct((steps, HD, QB), F32),
            jax.ShapeDtypeStruct((steps, length, QB), BF),
            jax.ShapeDtypeStruct((steps, 1, QB), F32),
        ],
        scratch_shapes=[pltpu.VMEM((HD, length), BF)],
        compiler_params=params(58, ("arbitrary",)),
        cost_estimate=pl.CostEstimate(
            flops=4 * length * length * HD, bytes_accessed=2 * length * length, transcendentals=length * length
        ),
        name="attend",
    )(spread, spread, spread)


def attend_back_kernel(
    q_ref, k_ref, v_ref, dout_ref, wide_ref, exps_ref, sums_ref, out_ref, kt_ref, dk_ref, dv_ref
):
    step = pl.program_id(0)
    groups, _, tok, _ = k_ref.shape
    per = QB // tok

    @pl.when(step == 0)
    def _():
        kt_ref[...] = k_ref[...].reshape(-1, HD).T
        dk_ref[...] = jnp.zeros_like(dk_ref)
        dv_ref[...] = jnp.zeros_like(dv_ref)

    queries = q_ref[...].reshape(QB, HD)
    dout = jnp.concatenate([dout_ref[p] for p in range(per)], axis=1)
    inv_sum = sums_ref[0]
    wide_dout = dout.astype(F32)
    dout_low = (wide_dout * inv_sum).astype(BF)
    centre = jnp.sum(wide_dout * wide_ref[0], axis=0, keepdims=True)
    factor = inv_sum * (1.0 / math.sqrt(HD))
    dq = 0.0
    for c in range(groups * tok // KB):
        at = slice(c * KB, (c + 1) * KB)
        values = v_ref[c * KB // tok : (c + 1) * KB // tok].reshape(KB, HD)
        low = exps_ref[0, at, :]
        dprobs = jnp.dot(values, dout, preferred_element_type=F32)
        dscores = (low.astype(F32) * ((dprobs - centre) * factor)).astype(BF)
        dv_ref[at, :] += lax.dot_general(
            low, dout_low, (((1,), (1,)), ((), ())), preferred_element_type=F32
        )
        dk_ref[at, :] += jnp.dot(dscores, queries, preferred_element_type=F32)
        dq += jnp.dot(kt_ref[:, at], dscores, preferred_element_type=F32)
    out_ref[pl.ds(step * per, per), 0] = dq.T.astype(BF).reshape(per, tok, HD)

    @pl.when(step == pl.num_programs(0) - 1)
    def _():
        out_ref[:, 1] = dk_ref[...].astype(BF).reshape(groups, tok, HD)
        out_ref[:, 2] = dv_ref[...].astype(BF).reshape(groups, tok, HD)


def attend_back(spread, dout, wide, exps, sums):
    groups, _, tok, _ = spread.shape
    length = groups * tok
    per = QB // tok
    steps = length // QB
    return pl.pallas_call(
        attend_back_kernel,
        grid=(steps,),
        in_specs=[
            pl.BlockSpec((per, 1, tok, HD), lambda i: (i, 0, 0, 0)),
            pl.BlockSpec((groups, 1, tok, HD), lambda i: (0, 1, 0, 0)),
            pl.BlockSpec((groups, 1, tok, HD), lambda i: (0, 2, 0, 0)),
            pl.BlockSpec((per, HD, tok), lambda i: (i, 0, 0)),
            pl.BlockSpec((1, HD, QB), lambda i: (i, 0, 0)),
            pl.BlockSpec((1, length, QB), lambda i: (i, 0, 0)),
            pl.BlockSpec((1, 1, QB), lambda i: (i, 0, 0)),
        ],
        out_specs=pl.BlockSpec((groups, 3, tok, HD), lambda i: (0, 0, 0, 0)),
        out_shape=jax.ShapeDtypeStruct((groups, 3, tok, HD), BF),
        scratch_shapes=[
            pltpu.VMEM((HD, length), BF),
            pltpu.VMEM((length, HD), F32),
            pltpu.VMEM((length, HD), F32),
        ],
        compiler_params=params(58, ("arbitrary",)),
        cost_estimate=pl.CostEstimate(
            flops=8 * length * length * HD, bytes_accessed=2 * length * length, transcendentals=0
        ),
        name="attend_back",
    )(spread, spread, spread, dout, wide, exps, sums)


def gather_block(order_ref, factor, j, source_ref):
    pieces = []
    for p in range(PER):
        at = pl.multiple_of(order_ref[factor, j * PER + p] * PIECE, PIECE)
        pieces.append(source_ref[pl.ds(at, PIECE), :])
    return jnp.concatenate(pieces, axis=0)


def scatter_block(order_ref, factor, j, block, target_ref):
    for p in range(PER):
        at = pl.multiple_of(order_ref[factor, j * PER + p] * PIECE, PIECE)
        target_ref[pl.ds(at, PIECE), :] = block[p * PIECE : (p + 1) * PIECE, :]


def down_kernel(order_ref, home_ref, cot_ref, near_ref, far_ref, moved_ref, up_ref, flip_ref, rot_ref, a_ref, b_ref):
    blocks = cot_ref.shape[1] // BS
    half = near_ref.shape[0]

    def place(i, carry):
        for base, source in ((0, near_ref), (half, far_ref)):
            rot = source[i]
            at = home_ref[base + i]
            rot_ref[at] = rot
            flip_ref[at] = rot.T
        return carry

    lax.fori_loop(0, half, place, 0, unroll=4)
    for j in range(blocks):
        a_ref[j * BS : (j + 1) * BS, :] = cot_ref[:, j * BS : (j + 1) * BS].T
    source, target = a_ref, b_ref
    for factor in reversed(range(FACTORS)):
        if factor == 0:
            target = up_ref

        def body(j, carry, factor=factor, source=source, target=target):
            block = gather_block(order_ref, factor, j, source)
            moved_ref[factor, pl.ds(pl.multiple_of(j * BS, BS), BS), :] = block
            back = jnp.dot(
                rot_ref[factor * blocks + j], block, preferred_element_type=F32
            ).astype(BF)
            scatter_block(order_ref, factor, j, back, target)
            return carry

        lax.fori_loop(0, blocks, body, 0, unroll=4)
        source, target = target, source


def down(orders, home, cotangent, near, far):
    tok, width = cotangent.shape
    total = 2 * near.shape[0]
    smem = pl.BlockSpec(memory_space=pltpu.SMEM)
    vmem = pl.BlockSpec(memory_space=pltpu.VMEM)
    return pl.pallas_call(
        down_kernel,
        in_specs=[smem, smem, vmem, vmem, vmem],
        out_specs=[vmem, vmem, vmem],
        out_shape=[
            jax.ShapeDtypeStruct((FACTORS, width, tok), BF),
            jax.ShapeDtypeStruct((width, tok), BF),
            jax.ShapeDtypeStruct((total, BS, BS), BF),
        ],
        scratch_shapes=[
            pltpu.VMEM((total, BS, BS), BF),
            pltpu.VMEM((width, tok), BF),
            pltpu.VMEM((width, tok), BF),
        ],
        compiler_params=params(40),
        cost_estimate=pl.CostEstimate(flops=10**9, bytes_accessed=10**7, transcendentals=0),
        name="butterfly_down",
    )(orders, home, cotangent, near, far)


def up_kernel(order_ref, self_ref, proj_ref, flip_ref, moved_ref, out_ref, mine_ref, other_ref, a_ref, b_ref):
    step = pl.program_id(0)
    width = proj_ref.shape[1]
    blocks = width // BS
    owned = mine_ref.shape[1]
    core = self_ref[2]
    factor, pair = step // 2, step % 2

    @pl.when(step == 0)
    def _():
        for j in range(blocks):
            a_ref[j * BS : (j + 1) * BS, :] = proj_ref[:, j * BS : (j + 1) * BS].T

    def turn_over(source, target):
        for half, grad_ref in ((core, mine_ref), (1 - core, other_ref)):
            for i in range(owned):
                inside = half * owned + i
                places = [
                    pl.multiple_of(
                        order_ref[factor, (2 * owned * pair + inside) * PER + p] * PIECE, PIECE
                    )
                    for p in range(PER)
                ]
                block = jnp.concatenate([source[pl.ds(at, PIECE), :] for at in places], axis=0)
                mixed = jnp.dot(flip_ref[inside], block, preferred_element_type=F32).astype(BF)
                for p, at in enumerate(places):
                    target[pl.ds(at, PIECE), :] = mixed[p * PIECE : (p + 1) * PIECE, :]
                moved = moved_ref[0, pl.ds(pl.multiple_of(inside * BS, BS), BS), :]
                grad_ref[0, i] = lax.dot_general(
                    block, moved, (((1,), (1,)), ((), ())), preferred_element_type=F32
                ).astype(BF)

    @pl.when(factor % 2 == 0)
    def _():
        turn_over(a_ref, b_ref)

    @pl.when(factor % 2 == 1)
    def _():
        turn_over(b_ref, a_ref)

    @pl.when(step == pl.num_programs(0) - 1)
    def _():
        for j in range(blocks):
            out_ref[:, j * BS : (j + 1) * BS] = a_ref[j * BS : (j + 1) * BS, :].T


def up(orders, position, projected, flipped, moved):
    tok, width = projected.shape
    owned = flipped.shape[0] // 16
    pairs = 8
    rows = FACTORS * width // pairs
    half = jax.ShapeDtypeStruct((pairs, owned, BS, BS), BF)

    def slot(t, order_ref, self_ref):
        return ((t // 4) ^ self_ref[0]) * 4 + (t % 4 + 4 - self_ref[1]) % 4, 0, 0, 0

    return pl.pallas_call(
        up_kernel,
        grid_spec=pltpu.PrefetchScalarGridSpec(
            num_scalar_prefetch=2,
            grid=(pairs,),
            in_specs=[
                pl.BlockSpec((tok, width), lambda t, *_: (0, 0)),
                pl.BlockSpec((2 * owned, BS, BS), lambda t, *_: (t, 0, 0)),
                pl.BlockSpec((1, rows, tok), lambda t, *_: (t, 0, 0)),
            ],
            out_specs=[
                pl.BlockSpec((tok, width), lambda t, *_: (0, 0)),
                pl.BlockSpec((1, owned, BS, BS), slot),
                pl.BlockSpec((1, owned, BS, BS), slot),
            ],
            scratch_shapes=[pltpu.VMEM((width, tok), BF), pltpu.VMEM((width, tok), BF)],
        ),
        out_shape=[jax.ShapeDtypeStruct((tok, width), BF), half, half],
        compiler_params=params(58, ("arbitrary",)),
        cost_estimate=pl.CostEstimate(flops=10**9, bytes_accessed=10**7, transcendentals=0),
        name="butterfly_up",
    )(orders, position, projected, flipped, moved.reshape(pairs, rows, tok))


def products_kernel(weight_ref, up_ref, att_ref, back_ref, proj_ref, acc_ref):
    step = pl.program_id(0)
    weight = weight_ref[...]
    back_ref[...] = jnp.dot(weight, up_ref[...], preferred_element_type=F32).astype(BF)
    att = jnp.concatenate([att_ref[p] for p in range(att_ref.shape[0])], axis=1)
    term = jnp.dot(att, weight, preferred_element_type=F32)

    @pl.when(step == 0)
    def _():
        acc_ref[...] = term

    @pl.when(step > 0)
    def _():
        acc_ref[...] += term

    @pl.when(step == pl.num_programs(0) - 1)
    def _():
        proj_ref[...] = acc_ref[...].astype(BF)


def products(weight, upstream, att):
    rows, width = weight.shape
    tok = upstream.shape[1]
    tile = 512
    return pl.pallas_call(
        products_kernel,
        grid=(rows // tile,),
        in_specs=[
            pl.BlockSpec((tile, width), lambda i: (i, 0)),
            pl.BlockSpec((width, tok), lambda i: (0, 0)),
            pl.BlockSpec((tile // HD, tok, HD), lambda i: (i, 0, 0)),
        ],
        out_specs=[
            pl.BlockSpec((tile, tok), lambda i: (i, 0)),
            pl.BlockSpec((tok, width), lambda i: (0, 0)),
        ],
        out_shape=[
            jax.ShapeDtypeStruct((rows, tok), BF),
            jax.ShapeDtypeStruct((tok, width), BF),
        ],
        scratch_shapes=[pltpu.VMEM((tok, width), F32)],
        compiler_params=params(58, ("arbitrary",)),
        cost_estimate=pl.CostEstimate(
            flops=4 * rows * width * tok, bytes_accessed=2 * rows * width, transcendentals=0
        ),
        name="products",
    )(weight, upstream, att)


def swap(x, axis):
    return lax.ppermute(x, axis, [(0, 1), (1, 0)])


def shift(x, axis, by):
    n = lax.axis_size(axis)
    return lax.ppermute(x, axis, [(i, (i + by) % n) for i in range(n)])


def turn(x, by):
    order = [(x_hi * 2 + x_lo) for x_lo in range(2) for x_hi in range(2)]
    at = {x: i for i, x in enumerate(order)}
    return lax.ppermute(x, ("xl", "xh"), [(at[i], at[(i + by) % 4]) for i in range(4)])


def cross(x):
    half = x.shape[0] // 2
    return jnp.concatenate([turn(x[:half], 1), turn(x[half:], 3)], axis=0)


def partner(x, axis, bit):
    return lax.ppermute(x, axis, [(i, i ^ bit) for i in range(lax.axis_size(axis))])


def add(*terms):
    return sum(t.astype(F32) for t in terms).astype(BF)


def after(x, *others):
    return lax.optimization_barrier((x,) + others)[0]


def gather_column(own):
    return jnp.concatenate([own, shift(own, "y", 1), shift(own, "y", 3), shift(own, "y", 2)], axis=0)


def gather_blocks(column, crossed):
    count = column.shape[0] // 4
    near = jnp.concatenate([column, crossed], axis=0)
    far = swap(near, "c")
    at = jnp.arange(16 * count, dtype=jnp.int32)
    slot, inside = at // count, at % count
    back = jnp.array([0, 1, 3, 2], jnp.int32)[slot % 4]
    y = (lax.axis_index("y") - back) % 4
    xl = lax.axis_index("xl") ^ ((slot // 4) % 2)
    c = lax.axis_index("c") ^ (slot // 8)
    return near, far, ((xl * 4 + y) * 2 + c) * count + inside


def local(attn_inputs, out_weight, skew_params, piece_orders, cotangent):
    tok = attn_inputs.shape[1]
    width = out_weight.shape[1]
    seqs = 16
    position = jnp.stack([lax.axis_index(a) for a in ROWS]).astype(jnp.int32)
    weight = lax.all_gather(out_weight, ROWS, axis=0, tiled=True)
    rows = attn_inputs[0].reshape(tok, 3, seqs, HD).transpose(2, 1, 0, 3)
    spread = lax.all_to_all(rows, SEQ, split_axis=0, concat_axis=0, tiled=True)
    inverse, rot_own = cayley(after(skew_params, rows))
    column = gather_column(rot_own)
    crossed = cross(column)
    spread, crossed = lax.optimization_barrier((spread, crossed))
    att, wide, exps, sums = attend(spread)
    att_own = lax.all_to_all(att, SEQ, split_axis=0, concat_axis=0, tiled=True)
    near, far, home = gather_blocks(column, crossed)
    moved_grad, upstream, flipped = down(piece_orders, home, cotangent[0], near, after(far, att))
    grad_att, projected = products(weight, upstream, att_own)
    dout = lax.all_to_all(
        grad_att.reshape(seqs, HD, tok), SEQ, split_axis=0, concat_axis=0, tiled=True
    )
    block_output, mine, other = up(piece_orders, position, projected, flipped, moved_grad)
    mine, other, dout = lax.optimization_barrier((mine, other, dout))
    from_core = swap(other, "c")
    grads = attend_back(spread, dout, wide, exps, sums)
    from_core, grads = lax.optimization_barrier((from_core, grads))
    grads = lax.all_to_all(grads, SEQ, split_axis=0, concat_axis=0, tiled=True)
    grad_inputs = grads.transpose(2, 1, 0, 3).reshape(1, tok, 3, seqs * HD)
    from_xl = cross(add(mine[4:], from_core[4:]))
    share = add(mine[:4], from_core[:4], from_xl)
    share = add(share[0], *[shift(share[dy], "y", dy) for dy in (2, 1, 3)])
    share = add(share, partner(share, "xh", 1))
    shape = share.shape
    parts = lax.all_to_all(
        after(share, grads).reshape(8, -1, BS), "z", split_axis=0, concat_axis=0, tiled=True
    )
    part = add(*[parts[i] for i in range(8)])
    copies = jnp.broadcast_to(part[None], parts.shape)
    owner_grad = lax.all_to_all(copies, "z", split_axis=0, concat_axis=0, tiled=True).reshape(shape)
    total_tokens = 16 * tok * seqs
    grad_skew = cayley_pullback(inverse, owner_grad, 1.0 / math.sqrt(total_tokens))
    return block_output[None], grad_inputs, grad_skew


def solution(mesh):
    fine = Mesh(mesh.devices.reshape(2, 4, 2, 2, 8), ROWS + SEQ)
    in_specs = (
        P(ROWS, SEQ, None, None),
        P(ROWS, None),
        P(ROWS, None, None),
        P(),
        P(ROWS, SEQ, None),
    )
    out_specs = (P(ROWS, SEQ, None), P(ROWS, SEQ, None, None), P(ROWS, None, None))
    return jax.shard_map(local, mesh=fine, in_specs=in_specs, out_specs=out_specs, check_vma=False)
```

```python
import functools
import math

import jax
import jax.numpy as jnp
from jax import lax
from jax.experimental import pallas as pl
from jax.experimental.pallas import tpu as pltpu
from jax.sharding import Mesh, PartitionSpec as P

HEADS = 16
HD = 128
BS = 128
FACTORS = 4
PIECE = 32
PER = BS // PIECE
BF = jnp.bfloat16
F32 = jnp.float32
HIGH = lax.Precision.HIGHEST
ROWS = ("xl", "y", "c")
SEQ = ("xh", "z")
QB = 512
KB = 2048
PANEL = 32
LOG2E = 1.4426950408889634
MIB = 1024 * 1024


def params(limit, semantics=None):
    return pltpu.CompilerParams(vmem_limit_bytes=limit * MIB, dimension_semantics=semantics)


def inverse_kernel(skew_ref, inv_ref, rot_ref):
    count, size, _ = skew_ref.shape
    row = lax.broadcasted_iota(jnp.int32, (size, size), 0)
    col = lax.broadcasted_iota(jnp.int32, (size, size), 1)
    eye = (row == col).astype(F32)
    eye_panel = eye[:PANEL]
    rowp = lax.broadcasted_iota(jnp.int32, (size, PANEL), 0)
    colp = lax.broadcasted_iota(jnp.int32, (size, PANEL), 1)
    for b in range(count):
        params_b = skew_ref[b]
        inv_ref[b] = eye + params_b - params_b.T

    def step(g, carry):
        first = pl.multiple_of(g * PANEL, PANEL)
        panels = [inv_ref[b, pl.ds(first, PANEL), :] for b in range(count)]
        sides = [eye_panel] * count
        for j in range(PANEL):
            pick = (lax.broadcasted_iota(jnp.int32, (PANEL, 1), 0) == j).astype(F32)
            for b in range(count):
                panel, side = panels[b], sides[b]
                scale = 1.0 / panel[j : j + 1, j : j + 1]
                left = panel[:, j : j + 1] - pick
                panels[b] = panel - left * (panel[j : j + 1, :] * scale)
                sides[b] = side - left * (side[j : j + 1, :] * scale)
        selector = (rowp - first == colp).astype(F32)
        for b in range(count):
            whole = inv_ref[b]
            update = jnp.dot(
                whole[:, :PANEL] - selector,
                panels[b] + sides[b],
                precision=HIGH,
                preferred_element_type=F32,
            )
            inv_ref[b] = pltpu.roll(whole - update, size - PANEL, 1)
        return carry

    lax.fori_loop(0, size // PANEL, step, 0)
    for b in range(count):
        rot_ref[b] = (2.0 * inv_ref[b] - eye).astype(BF)


def cayley(skew):
    return pl.pallas_call(
        inverse_kernel,
        out_shape=(
            jax.ShapeDtypeStruct(skew.shape, F32),
            jax.ShapeDtypeStruct(skew.shape, BF),
        ),
        compiler_params=params(32),
        name="cayley",
    )(skew)


def pullback_kernel(scaling, inv_ref, grad_ref, out_ref):
    for b in range(inv_ref.shape[0]):
        flipped = inv_ref[b].T
        grad = grad_ref[b].astype(F32) * (-2.0 * scaling)
        inner = jnp.dot(flipped, grad, precision=HIGH, preferred_element_type=F32)
        grad_s = jnp.dot(inner, flipped, precision=HIGH, preferred_element_type=F32)
        out_ref[b] = grad_s - grad_s.T


def cayley_pullback(inverse, grad, scaling):
    return pl.pallas_call(
        functools.partial(pullback_kernel, scaling),
        out_shape=jax.ShapeDtypeStruct(inverse.shape, F32),
        compiler_params=params(32),
        name="cayley_pullback",
    )(inverse, grad)


def attend_kernel(q_ref, k_ref, v_ref, att_ref, wide_ref, exps_ref, sums_ref, vt_ref):
    @pl.when(pl.program_id(0) == 0)
    def _():
        vt_ref[...] = v_ref[...].reshape(-1, HD).T

    queries = q_ref[...].reshape(QB, HD)
    groups, _, tok, _ = k_ref.shape
    length = groups * tok
    per = KB // tok
    factor = LOG2E / math.sqrt(HD)
    scores = []
    for c in range(length // KB):
        keys = k_ref[c * per : (c + 1) * per].reshape(KB, HD)
        scores.append(
            lax.dot_general(keys, queries, (((1,), (1,)), ((), ())), preferred_element_type=F32)
        )
    top = functools.reduce(jnp.maximum, [jnp.max(s, axis=0, keepdims=True) for s in scores])
    total, wide = 0.0, 0.0
    for c, part in enumerate(scores):
        exps = jnp.exp2((part - top) * factor)
        total += jnp.sum(exps, axis=0, keepdims=True)
        low = exps.astype(BF)
        exps_ref[0, c * KB : (c + 1) * KB, :] = low
        wide += jnp.dot(vt_ref[:, c * KB : (c + 1) * KB], low, preferred_element_type=F32)
    wide = wide / total
    wide_ref[0] = wide
    sums_ref[0] = 1.0 / total
    att_ref[...] = wide.T.astype(BF).reshape(att_ref.shape)


def attend(spread):
    groups, _, tok, _ = spread.shape
    length = groups * tok
    per = QB // tok
    steps = length // QB
    return pl.pallas_call(
        attend_kernel,
        grid=(steps,),
        in_specs=[
            pl.BlockSpec((per, 1, tok, HD), lambda i: (i, 0, 0, 0)),
            pl.BlockSpec((groups, 1, tok, HD), lambda i: (0, 1, 0, 0)),
            pl.BlockSpec((groups, 1, tok, HD), lambda i: (0, 2, 0, 0)),
        ],
        out_specs=[
            pl.BlockSpec((per, tok, HD), lambda i: (i, 0, 0)),
            pl.BlockSpec((1, HD, QB), lambda i: (i, 0, 0)),
            pl.BlockSpec((1, length, QB), lambda i: (i, 0, 0)),
            pl.BlockSpec((1, 1, QB), lambda i: (i, 0, 0)),
        ],
        out_shape=[
            jax.ShapeDtypeStruct((groups, tok, HD), BF),
            jax.ShapeDtypeStruct((steps, HD, QB), F32),
            jax.ShapeDtypeStruct((steps, length, QB), BF),
            jax.ShapeDtypeStruct((steps, 1, QB), F32),
        ],
        scratch_shapes=[pltpu.VMEM((HD, length), BF)],
        compiler_params=params(58, ("arbitrary",)),
        cost_estimate=pl.CostEstimate(
            flops=4 * length * length * HD, bytes_accessed=2 * length * length, transcendentals=length * length
        ),
        name="attend",
    )(spread, spread, spread)


def attend_back_kernel(
    q_ref, k_ref, v_ref, dout_ref, wide_ref, exps_ref, sums_ref, out_ref, kt_ref, dk_ref, dv_ref
):
    step = pl.program_id(0)
    groups, _, tok, _ = k_ref.shape
    per = QB // tok

    @pl.when(step == 0)
    def _():
        kt_ref[...] = k_ref[...].reshape(-1, HD).T
        dk_ref[...] = jnp.zeros_like(dk_ref)
        dv_ref[...] = jnp.zeros_like(dv_ref)

    queries = q_ref[...].reshape(QB, HD)
    dout = jnp.concatenate([dout_ref[p] for p in range(per)], axis=1)
    inv_sum = sums_ref[0]
    wide_dout = dout.astype(F32)
    dout_low = (wide_dout * inv_sum).astype(BF)
    centre = jnp.sum(wide_dout * wide_ref[0], axis=0, keepdims=True)
    factor = inv_sum * (1.0 / math.sqrt(HD))
    dq = 0.0
    for c in range(groups * tok // KB):
        at = slice(c * KB, (c + 1) * KB)
        values = v_ref[c * KB // tok : (c + 1) * KB // tok].reshape(KB, HD)
        low = exps_ref[0, at, :]
        dprobs = jnp.dot(values, dout, preferred_element_type=F32)
        dscores = (low.astype(F32) * ((dprobs - centre) * factor)).astype(BF)
        dv_ref[at, :] += lax.dot_general(
            low, dout_low, (((1,), (1,)), ((), ())), preferred_element_type=F32
        )
        dk_ref[at, :] += jnp.dot(dscores, queries, preferred_element_type=F32)
        dq += jnp.dot(kt_ref[:, at], dscores, preferred_element_type=F32)
    out_ref[pl.ds(step * per, per), 0] = dq.T.astype(BF).reshape(per, tok, HD)

    @pl.when(step == pl.num_programs(0) - 1)
    def _():
        out_ref[:, 1] = dk_ref[...].astype(BF).reshape(groups, tok, HD)
        out_ref[:, 2] = dv_ref[...].astype(BF).reshape(groups, tok, HD)


def attend_back(spread, dout, wide, exps, sums):
    groups, _, tok, _ = spread.shape
    length = groups * tok
    per = QB // tok
    steps = length // QB
    return pl.pallas_call(
        attend_back_kernel,
        grid=(steps,),
        in_specs=[
            pl.BlockSpec((per, 1, tok, HD), lambda i: (i, 0, 0, 0)),
            pl.BlockSpec((groups, 1, tok, HD), lambda i: (0, 1, 0, 0)),
            pl.BlockSpec((groups, 1, tok, HD), lambda i: (0, 2, 0, 0)),
            pl.BlockSpec((per, HD, tok), lambda i: (i, 0, 0)),
            pl.BlockSpec((1, HD, QB), lambda i: (i, 0, 0)),
            pl.BlockSpec((1, length, QB), lambda i: (i, 0, 0)),
            pl.BlockSpec((1, 1, QB), lambda i: (i, 0, 0)),
        ],
        out_specs=pl.BlockSpec((groups, 3, tok, HD), lambda i: (0, 0, 0, 0)),
        out_shape=jax.ShapeDtypeStruct((groups, 3, tok, HD), BF),
        scratch_shapes=[
            pltpu.VMEM((HD, length), BF),
            pltpu.VMEM((length, HD), F32),
            pltpu.VMEM((length, HD), F32),
        ],
        compiler_params=params(58, ("arbitrary",)),
        cost_estimate=pl.CostEstimate(
            flops=8 * length * length * HD, bytes_accessed=2 * length * length, transcendentals=0
        ),
        name="attend_back",
    )(spread, spread, spread, dout, wide, exps, sums)


def gather_block(order_ref, factor, j, source_ref):
    pieces = []
    for p in range(PER):
        at = pl.multiple_of(order_ref[factor, j * PER + p] * PIECE, PIECE)
        pieces.append(source_ref[pl.ds(at, PIECE), :])
    return jnp.concatenate(pieces, axis=0)


def scatter_block(order_ref, factor, j, block, target_ref):
    for p in range(PER):
        at = pl.multiple_of(order_ref[factor, j * PER + p] * PIECE, PIECE)
        target_ref[pl.ds(at, PIECE), :] = block[p * PIECE : (p + 1) * PIECE, :]


def down_kernel(order_ref, home_ref, cot_ref, near_ref, far_ref, moved_ref, up_ref, flip_ref, rot_ref, a_ref, b_ref):
    blocks = cot_ref.shape[1] // BS
    half = near_ref.shape[0]

    def place(i, carry):
        for base, source in ((0, near_ref), (half, far_ref)):
            rot = source[i]
            at = home_ref[base + i]
            rot_ref[at] = rot
            flip_ref[at] = rot.T
        return carry

    lax.fori_loop(0, half, place, 0, unroll=4)
    for j in range(blocks):
        a_ref[j * BS : (j + 1) * BS, :] = cot_ref[:, j * BS : (j + 1) * BS].T
    source, target = a_ref, b_ref
    for factor in reversed(range(FACTORS)):
        if factor == 0:
            target = up_ref

        def body(j, carry, factor=factor, source=source, target=target):
            block = gather_block(order_ref, factor, j, source)
            moved_ref[factor, pl.ds(pl.multiple_of(j * BS, BS), BS), :] = block
            back = jnp.dot(
                rot_ref[factor * blocks + j], block, preferred_element_type=F32
            ).astype(BF)
            scatter_block(order_ref, factor, j, back, target)
            return carry

        lax.fori_loop(0, blocks, body, 0, unroll=4)
        source, target = target, source


def down(orders, home, cotangent, near, far):
    tok, width = cotangent.shape
    total = 2 * near.shape[0]
    smem = pl.BlockSpec(memory_space=pltpu.SMEM)
    vmem = pl.BlockSpec(memory_space=pltpu.VMEM)
    return pl.pallas_call(
        down_kernel,
        in_specs=[smem, smem, vmem, vmem, vmem],
        out_specs=[vmem, vmem, vmem],
        out_shape=[
            jax.ShapeDtypeStruct((FACTORS, width, tok), BF),
            jax.ShapeDtypeStruct((width, tok), BF),
            jax.ShapeDtypeStruct((total, BS, BS), BF),
        ],
        scratch_shapes=[
            pltpu.VMEM((total, BS, BS), BF),
            pltpu.VMEM((width, tok), BF),
            pltpu.VMEM((width, tok), BF),
        ],
        compiler_params=params(40),
        cost_estimate=pl.CostEstimate(flops=10**9, bytes_accessed=10**7, transcendentals=0),
        name="butterfly_down",
    )(orders, home, cotangent, near, far)


def up_kernel(order_ref, self_ref, proj_ref, flip_ref, moved_ref, out_ref, mine_ref, other_ref, a_ref, b_ref):
    step = pl.program_id(0)
    width = proj_ref.shape[1]
    blocks = width // BS
    owned = mine_ref.shape[1]
    core = self_ref[2]
    factor, pair = step // 2, step % 2

    @pl.when(step == 0)
    def _():
        for j in range(blocks):
            a_ref[j * BS : (j + 1) * BS, :] = proj_ref[:, j * BS : (j + 1) * BS].T

    def turn_over(source, target):
        for half, grad_ref in ((core, mine_ref), (1 - core, other_ref)):
            for i in range(owned):
                inside = half * owned + i
                places = [
                    pl.multiple_of(
                        order_ref[factor, (2 * owned * pair + inside) * PER + p] * PIECE, PIECE
                    )
                    for p in range(PER)
                ]
                block = jnp.concatenate([source[pl.ds(at, PIECE), :] for at in places], axis=0)
                mixed = jnp.dot(flip_ref[inside], block, preferred_element_type=F32).astype(BF)
                for p, at in enumerate(places):
                    target[pl.ds(at, PIECE), :] = mixed[p * PIECE : (p + 1) * PIECE, :]
                moved = moved_ref[0, pl.ds(pl.multiple_of(inside * BS, BS), BS), :]
                grad_ref[0, i] = lax.dot_general(
                    block, moved, (((1,), (1,)), ((), ())), preferred_element_type=F32
                ).astype(BF)

    @pl.when(factor % 2 == 0)
    def _():
        turn_over(a_ref, b_ref)

    @pl.when(factor % 2 == 1)
    def _():
        turn_over(b_ref, a_ref)

    @pl.when(step == pl.num_programs(0) - 1)
    def _():
        for j in range(blocks):
            out_ref[:, j * BS : (j + 1) * BS] = a_ref[j * BS : (j + 1) * BS, :].T


def up(orders, position, projected, flipped, moved):
    tok, width = projected.shape
    owned = flipped.shape[0] // 16
    pairs = 8
    rows = FACTORS * width // pairs
    half = jax.ShapeDtypeStruct((pairs, owned, BS, BS), BF)

    def slot(t, order_ref, self_ref):
        return ((t // 4) ^ self_ref[0]) * 4 + (t % 4 + 4 - self_ref[1]) % 4, 0, 0, 0

    return pl.pallas_call(
        up_kernel,
        grid_spec=pltpu.PrefetchScalarGridSpec(
            num_scalar_prefetch=2,
            grid=(pairs,),
            in_specs=[
                pl.BlockSpec((tok, width), lambda t, *_: (0, 0)),
                pl.BlockSpec((2 * owned, BS, BS), lambda t, *_: (t, 0, 0)),
                pl.BlockSpec((1, rows, tok), lambda t, *_: (t, 0, 0)),
            ],
            out_specs=[
                pl.BlockSpec((tok, width), lambda t, *_: (0, 0)),
                pl.BlockSpec((1, owned, BS, BS), slot),
                pl.BlockSpec((1, owned, BS, BS), slot),
            ],
            scratch_shapes=[pltpu.VMEM((width, tok), BF), pltpu.VMEM((width, tok), BF)],
        ),
        out_shape=[jax.ShapeDtypeStruct((tok, width), BF), half, half],
        compiler_params=params(58, ("arbitrary",)),
        cost_estimate=pl.CostEstimate(flops=10**9, bytes_accessed=10**7, transcendentals=0),
        name="butterfly_up",
    )(orders, position, projected, flipped, moved.reshape(pairs, rows, tok))


def products_kernel(weight_ref, up_ref, att_ref, back_ref, proj_ref, acc_ref):
    step = pl.program_id(0)
    weight = weight_ref[...]
    back_ref[...] = jnp.dot(weight, up_ref[...], preferred_element_type=F32).astype(BF)
    att = jnp.concatenate([att_ref[p] for p in range(att_ref.shape[0])], axis=1)
    term = jnp.dot(att, weight, preferred_element_type=F32)

    @pl.when(step == 0)
    def _():
        acc_ref[...] = term

    @pl.when(step > 0)
    def _():
        acc_ref[...] += term

    @pl.when(step == pl.num_programs(0) - 1)
    def _():
        proj_ref[...] = acc_ref[...].astype(BF)


def products(weight, upstream, att):
    rows, width = weight.shape
    tok = upstream.shape[1]
    tile = 512
    return pl.pallas_call(
        products_kernel,
        grid=(rows // tile,),
        in_specs=[
            pl.BlockSpec((tile, width), lambda i: (i, 0)),
            pl.BlockSpec((width, tok), lambda i: (0, 0)),
            pl.BlockSpec((tile // HD, tok, HD), lambda i: (i, 0, 0)),
        ],
        out_specs=[
            pl.BlockSpec((tile, tok), lambda i: (i, 0)),
            pl.BlockSpec((tok, width), lambda i: (0, 0)),
        ],
        out_shape=[
            jax.ShapeDtypeStruct((rows, tok), BF),
            jax.ShapeDtypeStruct((tok, width), BF),
        ],
        scratch_shapes=[pltpu.VMEM((tok, width), F32)],
        compiler_params=params(58, ("arbitrary",)),
        cost_estimate=pl.CostEstimate(
            flops=4 * rows * width * tok, bytes_accessed=2 * rows * width, transcendentals=0
        ),
        name="products",
    )(weight, upstream, att)


def swap(x, axis):
    return lax.ppermute(x, axis, [(0, 1), (1, 0)])


def shift(x, axis, by):
    n = lax.axis_size(axis)
    return lax.ppermute(x, axis, [(i, (i + by) % n) for i in range(n)])


def turn(x, by):
    order = [(x_hi * 2 + x_lo) for x_lo in range(2) for x_hi in range(2)]
    at = {x: i for i, x in enumerate(order)}
    return lax.ppermute(x, ("xl", "xh"), [(at[i], at[(i + by) % 4]) for i in range(4)])


def cross(x):
    half = x.shape[0] // 2
    return jnp.concatenate([turn(x[:half], 1), turn(x[half:], 3)], axis=0)


def partner(x, axis, bit):
    return lax.ppermute(x, axis, [(i, i ^ bit) for i in range(lax.axis_size(axis))])


def add(*terms):
    return sum(t.astype(F32) for t in terms).astype(BF)


def after(x, *others):
    return lax.optimization_barrier((x,) + others)[0]


def gather_column(own):
    half = own.shape[0] // 2
    before, behind = shift(own, "y", 1), shift(own, "y", 3)
    across = [shift(before[:half], "y", 1), shift(behind[half:], "y", 3)]
    return jnp.concatenate([own, before, behind] + across, axis=0)


def gather_blocks(column, crossed):
    count = column.shape[0] // 4
    near = jnp.concatenate([column, crossed], axis=0)
    far = swap(near, "c")
    at = jnp.arange(16 * count, dtype=jnp.int32)
    slot, inside = at // count, at % count
    back = jnp.array([0, 1, 3, 2], jnp.int32)[slot % 4]
    y = (lax.axis_index("y") - back) % 4
    xl = lax.axis_index("xl") ^ ((slot // 4) % 2)
    c = lax.axis_index("c") ^ (slot // 8)
    return near, far, ((xl * 4 + y) * 2 + c) * count + inside


def local(attn_inputs, out_weight, skew_params, piece_orders, cotangent):
    tok = attn_inputs.shape[1]
    width = out_weight.shape[1]
    seqs = 16
    position = jnp.stack([lax.axis_index(a) for a in ROWS]).astype(jnp.int32)
    weight = lax.all_gather(out_weight, ROWS, axis=0, tiled=True)
    rows = attn_inputs[0].reshape(tok, 3, seqs, HD).transpose(2, 1, 0, 3)
    spread = lax.all_to_all(rows, SEQ, split_axis=0, concat_axis=0, tiled=True)
    inverse, rot_own = cayley(after(skew_params, rows))
    column = gather_column(rot_own)
    crossed = cross(column)
    spread, crossed = lax.optimization_barrier((spread, crossed))
    att, wide, exps, sums = attend(spread)
    att_own = lax.all_to_all(att, SEQ, split_axis=0, concat_axis=0, tiled=True)
    near, far, home = gather_blocks(column, crossed)
    moved_grad, upstream, flipped = down(piece_orders, home, cotangent[0], near, after(far, att))
    grad_att, projected = products(weight, upstream, att_own)
    dout = lax.all_to_all(
        grad_att.reshape(seqs, HD, tok), SEQ, split_axis=0, concat_axis=0, tiled=True
    )
    block_output, mine, other = up(piece_orders, position, projected, flipped, moved_grad)
    mine, other, dout = lax.optimization_barrier((mine, other, dout))
    from_core = swap(other, "c")
    grads = attend_back(spread, dout, wide, exps, sums)
    from_core, grads = lax.optimization_barrier((from_core, grads))
    grads = lax.all_to_all(grads, SEQ, split_axis=0, concat_axis=0, tiled=True)
    grad_inputs = grads.transpose(2, 1, 0, 3).reshape(1, tok, 3, seqs * HD)
    from_xl = cross(add(mine[4:], from_core[4:]))
    share = add(mine[:4], from_core[:4], from_xl)
    share = add(share[0], *[shift(share[dy], "y", dy) for dy in (2, 1, 3)])
    shape = share.shape
    parts = lax.all_to_all(
        after(share, grads).reshape(seqs, -1, BS), SEQ, split_axis=0, concat_axis=0, tiled=True
    )
    part = add(*[parts[i] for i in range(seqs)])
    copies = jnp.broadcast_to(part[None], parts.shape)
    owner_grad = lax.all_to_all(copies, SEQ, split_axis=0, concat_axis=0, tiled=True).reshape(shape)
    total_tokens = 16 * tok * seqs
    grad_skew = cayley_pullback(inverse, owner_grad, 1.0 / math.sqrt(total_tokens))
    return block_output[None], grad_inputs, grad_skew


def solution(mesh):
    fine = Mesh(mesh.devices.reshape(2, 4, 2, 2, 8), ROWS + SEQ)
    in_specs = (
        P(ROWS, SEQ, None, None),
        P(ROWS, None),
        P(ROWS, None, None),
        P(),
        P(ROWS, SEQ, None),
    )
    out_specs = (P(ROWS, SEQ, None), P(ROWS, SEQ, None, None), P(ROWS, None, None))
    return jax.shard_map(local, mesh=fine, in_specs=in_specs, out_specs=out_specs, check_vma=False)
```

```python
import functools
import math

import jax
import jax.numpy as jnp
from jax import lax
from jax.experimental import pallas as pl
from jax.experimental.pallas import tpu as pltpu
from jax.sharding import Mesh, PartitionSpec as P

HEADS = 16
HD = 128
BS = 128
FACTORS = 4
PIECE = 32
PER = BS // PIECE
BF = jnp.bfloat16
F32 = jnp.float32
HIGH = lax.Precision.HIGHEST
ROWS = ("xl", "y", "c")
SEQ = ("xh", "z")
QB = 512
KB = 2048
PANEL = 32
LOG2E = 1.4426950408889634
MIB = 1024 * 1024


def params(limit, semantics=None):
    return pltpu.CompilerParams(vmem_limit_bytes=limit * MIB, dimension_semantics=semantics)


def inverse_kernel(skew_ref, inv_ref, rot_ref):
    count, size, _ = skew_ref.shape
    row = lax.broadcasted_iota(jnp.int32, (size, size), 0)
    col = lax.broadcasted_iota(jnp.int32, (size, size), 1)
    eye = (row == col).astype(F32)
    eye_panel = eye[:PANEL]
    rowp = lax.broadcasted_iota(jnp.int32, (size, PANEL), 0)
    colp = lax.broadcasted_iota(jnp.int32, (size, PANEL), 1)
    for b in range(count):
        params_b = skew_ref[b]
        inv_ref[b] = eye + params_b - params_b.T

    def step(g, carry):
        first = pl.multiple_of(g * PANEL, PANEL)
        panels = [inv_ref[b, pl.ds(first, PANEL), :] for b in range(count)]
        sides = [eye_panel] * count
        for j in range(PANEL):
            pick = (lax.broadcasted_iota(jnp.int32, (PANEL, 1), 0) == j).astype(F32)
            for b in range(count):
                panel, side = panels[b], sides[b]
                scale = 1.0 / panel[j : j + 1, j : j + 1]
                left = panel[:, j : j + 1] - pick
                panels[b] = panel - left * (panel[j : j + 1, :] * scale)
                sides[b] = side - left * (side[j : j + 1, :] * scale)
        selector = (rowp - first == colp).astype(F32)
        for b in range(count):
            whole = inv_ref[b]
            update = jnp.dot(
                whole[:, :PANEL] - selector,
                panels[b] + sides[b],
                precision=HIGH,
                preferred_element_type=F32,
            )
            inv_ref[b] = pltpu.roll(whole - update, size - PANEL, 1)
        return carry

    lax.fori_loop(0, size // PANEL, step, 0)
    for b in range(count):
        rot_ref[b] = (2.0 * inv_ref[b] - eye).astype(BF)


def cayley(skew):
    return pl.pallas_call(
        inverse_kernel,
        out_shape=(
            jax.ShapeDtypeStruct(skew.shape, F32),
            jax.ShapeDtypeStruct(skew.shape, BF),
        ),
        compiler_params=params(32),
        name="cayley",
    )(skew)


def pullback_kernel(scaling, inv_ref, grad_ref, out_ref):
    for b in range(inv_ref.shape[0]):
        flipped = inv_ref[b].T
        grad = grad_ref[b].astype(F32) * (-2.0 * scaling)
        inner = jnp.dot(flipped, grad, precision=HIGH, preferred_element_type=F32)
        grad_s = jnp.dot(inner, flipped, precision=HIGH, preferred_element_type=F32)
        out_ref[b] = grad_s - grad_s.T


def cayley_pullback(inverse, grad, scaling):
    return pl.pallas_call(
        functools.partial(pullback_kernel, scaling),
        out_shape=jax.ShapeDtypeStruct(inverse.shape, F32),
        compiler_params=params(32),
        name="cayley_pullback",
    )(inverse, grad)


def attend_kernel(q_ref, k_ref, v_ref, att_ref, wide_ref, exps_ref, sums_ref, vt_ref):
    @pl.when(pl.program_id(0) == 0)
    def _():
        vt_ref[...] = v_ref[...].reshape(-1, HD).T

    queries = q_ref[...].reshape(QB, HD)
    groups, _, tok, _ = k_ref.shape
    length = groups * tok
    per = KB // tok
    factor = LOG2E / math.sqrt(HD)
    scores = []
    for c in range(length // KB):
        keys = k_ref[c * per : (c + 1) * per].reshape(KB, HD)
        scores.append(
            lax.dot_general(keys, queries, (((1,), (1,)), ((), ())), preferred_element_type=F32)
        )
    top = functools.reduce(jnp.maximum, [jnp.max(s, axis=0, keepdims=True) for s in scores])
    total, wide = 0.0, 0.0
    for c, part in enumerate(scores):
        exps = jnp.exp2((part - top) * factor)
        total += jnp.sum(exps, axis=0, keepdims=True)
        low = exps.astype(BF)
        exps_ref[0, c * KB : (c + 1) * KB, :] = low
        wide += jnp.dot(vt_ref[:, c * KB : (c + 1) * KB], low, preferred_element_type=F32)
    wide = wide / total
    wide_ref[0] = wide
    sums_ref[0] = 1.0 / total
    att_ref[...] = wide.T.astype(BF).reshape(att_ref.shape)


def attend(spread):
    groups, _, tok, _ = spread.shape
    length = groups * tok
    per = QB // tok
    steps = length // QB
    return pl.pallas_call(
        attend_kernel,
        grid=(steps,),
        in_specs=[
            pl.BlockSpec((per, 1, tok, HD), lambda i: (i, 0, 0, 0)),
            pl.BlockSpec((groups, 1, tok, HD), lambda i: (0, 1, 0, 0)),
            pl.BlockSpec((groups, 1, tok, HD), lambda i: (0, 2, 0, 0)),
        ],
        out_specs=[
            pl.BlockSpec((per, tok, HD), lambda i: (i, 0, 0)),
            pl.BlockSpec((1, HD, QB), lambda i: (i, 0, 0)),
            pl.BlockSpec((1, length, QB), lambda i: (i, 0, 0)),
            pl.BlockSpec((1, 1, QB), lambda i: (i, 0, 0)),
        ],
        out_shape=[
            jax.ShapeDtypeStruct((groups, tok, HD), BF),
            jax.ShapeDtypeStruct((steps, HD, QB), F32),
            jax.ShapeDtypeStruct((steps, length, QB), BF),
            jax.ShapeDtypeStruct((steps, 1, QB), F32),
        ],
        scratch_shapes=[pltpu.VMEM((HD, length), BF)],
        compiler_params=params(63, ("arbitrary",)),
        cost_estimate=pl.CostEstimate(
            flops=4 * length * length * HD, bytes_accessed=2 * length * length, transcendentals=length * length
        ),
        name="attend",
    )(spread, spread, spread)


def attend_back_kernel(
    q_ref, k_ref, v_ref, dout_ref, wide_ref, exps_ref, sums_ref, out_ref, kt_ref, dk_ref, dv_ref
):
    step = pl.program_id(0)
    groups, _, tok, _ = k_ref.shape
    per = QB // tok

    @pl.when(step == 0)
    def _():
        kt_ref[...] = k_ref[...].reshape(-1, HD).T
        dk_ref[...] = jnp.zeros_like(dk_ref)
        dv_ref[...] = jnp.zeros_like(dv_ref)

    queries = q_ref[...].reshape(QB, HD)
    dout = jnp.concatenate([dout_ref[p] for p in range(per)], axis=1)
    inv_sum = sums_ref[0]
    wide_dout = dout.astype(F32)
    dout_low = (wide_dout * inv_sum).astype(BF)
    centre = jnp.sum(wide_dout * wide_ref[0], axis=0, keepdims=True)
    factor = inv_sum * (1.0 / math.sqrt(HD))
    dq = 0.0
    for c in range(groups * tok // KB):
        at = slice(c * KB, (c + 1) * KB)
        values = v_ref[c * KB // tok : (c + 1) * KB // tok].reshape(KB, HD)
        low = exps_ref[0, at, :]
        dprobs = jnp.dot(values, dout, preferred_element_type=F32)
        dscores = (low.astype(F32) * ((dprobs - centre) * factor)).astype(BF)
        dv_ref[at, :] += lax.dot_general(
            low, dout_low, (((1,), (1,)), ((), ())), preferred_element_type=F32
        )
        dk_ref[at, :] += jnp.dot(dscores, queries, preferred_element_type=F32)
        dq += jnp.dot(kt_ref[:, at], dscores, preferred_element_type=F32)
    out_ref[pl.ds(step * per, per), 0] = dq.T.astype(BF).reshape(per, tok, HD)

    @pl.when(step == pl.num_programs(0) - 1)
    def _():
        out_ref[:, 1] = dk_ref[...].astype(BF).reshape(groups, tok, HD)
        out_ref[:, 2] = dv_ref[...].astype(BF).reshape(groups, tok, HD)


def attend_back(spread, dout, wide, exps, sums):
    groups, _, tok, _ = spread.shape
    length = groups * tok
    per = QB // tok
    steps = length // QB
    return pl.pallas_call(
        attend_back_kernel,
        grid=(steps,),
        in_specs=[
            pl.BlockSpec((per, 1, tok, HD), lambda i: (i, 0, 0, 0)),
            pl.BlockSpec((groups, 1, tok, HD), lambda i: (0, 1, 0, 0)),
            pl.BlockSpec((groups, 1, tok, HD), lambda i: (0, 2, 0, 0)),
            pl.BlockSpec((per, HD, tok), lambda i: (i, 0, 0)),
            pl.BlockSpec((1, HD, QB), lambda i: (i, 0, 0)),
            pl.BlockSpec((1, length, QB), lambda i: (i, 0, 0)),
            pl.BlockSpec((1, 1, QB), lambda i: (i, 0, 0)),
        ],
        out_specs=pl.BlockSpec((groups, 3, tok, HD), lambda i: (0, 0, 0, 0)),
        out_shape=jax.ShapeDtypeStruct((groups, 3, tok, HD), BF),
        scratch_shapes=[
            pltpu.VMEM((HD, length), BF),
            pltpu.VMEM((length, HD), F32),
            pltpu.VMEM((length, HD), F32),
        ],
        compiler_params=params(63, ("arbitrary",)),
        cost_estimate=pl.CostEstimate(
            flops=8 * length * length * HD, bytes_accessed=2 * length * length, transcendentals=0
        ),
        name="attend_back",
    )(spread, spread, spread, dout, wide, exps, sums)


def gather_block(order_ref, factor, j, source_ref):
    pieces = []
    for p in range(PER):
        at = pl.multiple_of(order_ref[factor, j * PER + p] * PIECE, PIECE)
        pieces.append(source_ref[pl.ds(at, PIECE), :])
    return jnp.concatenate(pieces, axis=0)


def scatter_block(order_ref, factor, j, block, target_ref):
    for p in range(PER):
        at = pl.multiple_of(order_ref[factor, j * PER + p] * PIECE, PIECE)
        target_ref[pl.ds(at, PIECE), :] = block[p * PIECE : (p + 1) * PIECE, :]


def down_kernel(order_ref, home_ref, cot_ref, near_ref, far_ref, moved_ref, up_ref, flip_ref, rot_ref, a_ref, b_ref):
    blocks = cot_ref.shape[1] // BS
    half = near_ref.shape[0]

    def place(i, carry):
        for base, source in ((0, near_ref), (half, far_ref)):
            rot = source[i]
            at = home_ref[base + i]
            rot_ref[at] = rot
            flip_ref[at] = rot.T
        return carry

    lax.fori_loop(0, half, place, 0, unroll=4)
    for j in range(blocks):
        a_ref[j * BS : (j + 1) * BS, :] = cot_ref[:, j * BS : (j + 1) * BS].T
    source, target = a_ref, b_ref
    for factor in reversed(range(FACTORS)):
        if factor == 0:
            target = up_ref

        def body(j, carry, factor=factor, source=source, target=target):
            block = gather_block(order_ref, factor, j, source)
            moved_ref[factor, pl.ds(pl.multiple_of(j * BS, BS), BS), :] = block
            back = jnp.dot(
                rot_ref[factor * blocks + j], block, preferred_element_type=F32
            ).astype(BF)
            scatter_block(order_ref, factor, j, back, target)
            return carry

        lax.fori_loop(0, blocks, body, 0, unroll=4)
        source, target = target, source


def down(orders, home, cotangent, near, far):
    tok, width = cotangent.shape
    total = 2 * near.shape[0]
    smem = pl.BlockSpec(memory_space=pltpu.SMEM)
    vmem = pl.BlockSpec(memory_space=pltpu.VMEM)
    return pl.pallas_call(
        down_kernel,
        in_specs=[smem, smem, vmem, vmem, vmem],
        out_specs=[vmem, vmem, vmem],
        out_shape=[
            jax.ShapeDtypeStruct((FACTORS, width, tok), BF),
            jax.ShapeDtypeStruct((width, tok), BF),
            jax.ShapeDtypeStruct((total, BS, BS), BF),
        ],
        scratch_shapes=[
            pltpu.VMEM((total, BS, BS), BF),
            pltpu.VMEM((width, tok), BF),
            pltpu.VMEM((width, tok), BF),
        ],
        compiler_params=params(40),
        cost_estimate=pl.CostEstimate(flops=10**9, bytes_accessed=10**7, transcendentals=0),
        name="butterfly_down",
    )(orders, home, cotangent, near, far)


def up_kernel(order_ref, self_ref, proj_ref, flip_ref, moved_ref, out_ref, mine_ref, other_ref, a_ref, b_ref):
    step = pl.program_id(0)
    width = proj_ref.shape[1]
    blocks = width // BS
    owned = mine_ref.shape[1]
    core = self_ref[2]
    factor, pair = step // 2, step % 2

    @pl.when(step == 0)
    def _():
        for j in range(blocks):
            a_ref[j * BS : (j + 1) * BS, :] = proj_ref[:, j * BS : (j + 1) * BS].T

    def turn_over(source, target):
        for half, grad_ref in ((core, mine_ref), (1 - core, other_ref)):
            for i in range(owned):
                inside = half * owned + i
                places = [
                    pl.multiple_of(
                        order_ref[factor, (2 * owned * pair + inside) * PER + p] * PIECE, PIECE
                    )
                    for p in range(PER)
                ]
                block = jnp.concatenate([source[pl.ds(at, PIECE), :] for at in places], axis=0)
                mixed = jnp.dot(flip_ref[inside], block, preferred_element_type=F32).astype(BF)
                for p, at in enumerate(places):
                    target[pl.ds(at, PIECE), :] = mixed[p * PIECE : (p + 1) * PIECE, :]
                moved = moved_ref[0, pl.ds(pl.multiple_of(inside * BS, BS), BS), :]
                grad_ref[0, i] = lax.dot_general(
                    block, moved, (((1,), (1,)), ((), ())), preferred_element_type=F32
                ).astype(BF)

    @pl.when(factor % 2 == 0)
    def _():
        turn_over(a_ref, b_ref)

    @pl.when(factor % 2 == 1)
    def _():
        turn_over(b_ref, a_ref)

    @pl.when(step == pl.num_programs(0) - 1)
    def _():
        for j in range(blocks):
            out_ref[:, j * BS : (j + 1) * BS] = a_ref[j * BS : (j + 1) * BS, :].T


def up(orders, position, projected, flipped, moved):
    tok, width = projected.shape
    owned = flipped.shape[0] // 16
    pairs = 8
    rows = FACTORS * width // pairs
    half = jax.ShapeDtypeStruct((pairs, owned, BS, BS), BF)

    def slot(t, order_ref, self_ref):
        return ((t // 4) ^ self_ref[0]) * 4 + (t % 4 + 4 - self_ref[1]) % 4, 0, 0, 0

    return pl.pallas_call(
        up_kernel,
        grid_spec=pltpu.PrefetchScalarGridSpec(
            num_scalar_prefetch=2,
            grid=(pairs,),
            in_specs=[
                pl.BlockSpec((tok, width), lambda t, *_: (0, 0)),
                pl.BlockSpec((2 * owned, BS, BS), lambda t, *_: (t, 0, 0)),
                pl.BlockSpec((1, rows, tok), lambda t, *_: (t, 0, 0)),
            ],
            out_specs=[
                pl.BlockSpec((tok, width), lambda t, *_: (0, 0)),
                pl.BlockSpec((1, owned, BS, BS), slot),
                pl.BlockSpec((1, owned, BS, BS), slot),
            ],
            scratch_shapes=[pltpu.VMEM((width, tok), BF), pltpu.VMEM((width, tok), BF)],
        ),
        out_shape=[jax.ShapeDtypeStruct((tok, width), BF), half, half],
        compiler_params=params(63, ("arbitrary",)),
        cost_estimate=pl.CostEstimate(flops=10**9, bytes_accessed=10**7, transcendentals=0),
        name="butterfly_up",
    )(orders, position, projected, flipped, moved.reshape(pairs, rows, tok))


def products_kernel(weight_ref, up_ref, att_ref, back_ref, proj_ref, acc_ref):
    step = pl.program_id(0)
    weight = weight_ref[...]
    back_ref[...] = jnp.dot(weight, up_ref[...], preferred_element_type=F32).astype(BF)
    att = jnp.concatenate([att_ref[p] for p in range(att_ref.shape[0])], axis=1)
    term = jnp.dot(att, weight, preferred_element_type=F32)

    @pl.when(step == 0)
    def _():
        acc_ref[...] = term

    @pl.when(step > 0)
    def _():
        acc_ref[...] += term

    @pl.when(step == pl.num_programs(0) - 1)
    def _():
        proj_ref[...] = acc_ref[...].astype(BF)


def products(weight, upstream, att):
    rows, width = weight.shape
    tok = upstream.shape[1]
    tile = 512
    return pl.pallas_call(
        products_kernel,
        grid=(rows // tile,),
        in_specs=[
            pl.BlockSpec((tile, width), lambda i: (i, 0)),
            pl.BlockSpec((width, tok), lambda i: (0, 0)),
            pl.BlockSpec((tile // HD, tok, HD), lambda i: (i, 0, 0)),
        ],
        out_specs=[
            pl.BlockSpec((tile, tok), lambda i: (i, 0)),
            pl.BlockSpec((tok, width), lambda i: (0, 0)),
        ],
        out_shape=[
            jax.ShapeDtypeStruct((rows, tok), BF),
            jax.ShapeDtypeStruct((tok, width), BF),
        ],
        scratch_shapes=[pltpu.VMEM((tok, width), F32)],
        compiler_params=params(63, ("arbitrary",)),
        cost_estimate=pl.CostEstimate(
            flops=4 * rows * width * tok, bytes_accessed=2 * rows * width, transcendentals=0
        ),
        name="products",
    )(weight, upstream, att)


def swap(x, axis):
    return lax.ppermute(x, axis, [(0, 1), (1, 0)])


def shift(x, axis, by):
    n = lax.axis_size(axis)
    return lax.ppermute(x, axis, [(i, (i + by) % n) for i in range(n)])


def turn(x, by):
    order = [(x_hi * 2 + x_lo) for x_lo in range(2) for x_hi in range(2)]
    at = {x: i for i, x in enumerate(order)}
    return lax.ppermute(x, ("xl", "xh"), [(at[i], at[(i + by) % 4]) for i in range(4)])


def cross(x):
    half = x.shape[0] // 2
    return jnp.concatenate([turn(x[:half], 1), turn(x[half:], 3)], axis=0)


def partner(x, axis, bit):
    return lax.ppermute(x, axis, [(i, i ^ bit) for i in range(lax.axis_size(axis))])


def add(*terms):
    return sum(t.astype(F32) for t in terms).astype(BF)


def after(x, *others):
    return lax.optimization_barrier((x,) + others)[0]


def gather_column(own):
    half = own.shape[0] // 2
    before, behind = shift(own, "y", 1), shift(own, "y", 3)
    across = [shift(before[:half], "y", 1), shift(behind[half:], "y", 3)]
    return jnp.concatenate([own, before, behind] + across, axis=0)


def gather_blocks(column, crossed):
    count = column.shape[0] // 4
    near = jnp.concatenate([column, crossed], axis=0)
    far = swap(near, "c")
    at = jnp.arange(16 * count, dtype=jnp.int32)
    slot, inside = at // count, at % count
    back = jnp.array([0, 1, 3, 2], jnp.int32)[slot % 4]
    y = (lax.axis_index("y") - back) % 4
    xl = lax.axis_index("xl") ^ ((slot // 4) % 2)
    c = lax.axis_index("c") ^ (slot // 8)
    return near, far, ((xl * 4 + y) * 2 + c) * count + inside


def local(attn_inputs, out_weight, skew_params, piece_orders, cotangent):
    tok = attn_inputs.shape[1]
    width = out_weight.shape[1]
    seqs = 16
    position = jnp.stack([lax.axis_index(a) for a in ROWS]).astype(jnp.int32)
    weight = lax.all_gather(out_weight, ROWS, axis=0, tiled=True)
    rows = attn_inputs[0].reshape(tok, 3, seqs, HD).transpose(2, 1, 0, 3)
    spread = lax.all_to_all(rows, SEQ, split_axis=0, concat_axis=0, tiled=True)
    inverse, rot_own = cayley(after(skew_params, rows))
    column = gather_column(rot_own)
    crossed = cross(column)
    spread, crossed = lax.optimization_barrier((spread, crossed))
    att, wide, exps, sums = attend(spread)
    att_own = lax.all_to_all(att, SEQ, split_axis=0, concat_axis=0, tiled=True)
    near, far, home = gather_blocks(column, crossed)
    moved_grad, upstream, flipped = down(piece_orders, home, cotangent[0], near, after(far, att))
    grad_att, projected = products(weight, upstream, att_own)
    dout = lax.all_to_all(
        grad_att.reshape(seqs, HD, tok), SEQ, split_axis=0, concat_axis=0, tiled=True
    )
    block_output, mine, other = up(piece_orders, position, projected, flipped, moved_grad)
    mine, other, dout = lax.optimization_barrier((mine, other, dout))
    from_core = swap(other, "c")
    grads = attend_back(spread, dout, wide, exps, sums)
    from_core, grads = lax.optimization_barrier((from_core, grads))
    grads = lax.all_to_all(grads, SEQ, split_axis=0, concat_axis=0, tiled=True)
    grad_inputs = grads.transpose(2, 1, 0, 3).reshape(1, tok, 3, seqs * HD)
    from_xl = cross(add(mine[4:], from_core[4:]))
    share = add(mine[:4], from_core[:4], from_xl)
    share = add(share[0], *[shift(share[dy], "y", dy) for dy in (2, 1, 3)])
    shape = share.shape
    parts = lax.all_to_all(
        after(share, grads).reshape(seqs, -1, BS), SEQ, split_axis=0, concat_axis=0, tiled=True
    )
    part = add(*[parts[i] for i in range(seqs)])
    copies = jnp.broadcast_to(part[None], parts.shape)
    owner_grad = lax.all_to_all(copies, SEQ, split_axis=0, concat_axis=0, tiled=True).reshape(shape)
    total_tokens = 16 * tok * seqs
    grad_skew = cayley_pullback(inverse, owner_grad, 1.0 / math.sqrt(total_tokens))
    return block_output[None], grad_inputs, grad_skew


def solution(mesh):
    fine = Mesh(mesh.devices.reshape(2, 4, 2, 2, 8), ROWS + SEQ)
    in_specs = (
        P(ROWS, SEQ, None, None),
        P(ROWS, None),
        P(ROWS, None, None),
        P(),
        P(ROWS, SEQ, None),
    )
    out_specs = (P(ROWS, SEQ, None), P(ROWS, SEQ, None, None), P(ROWS, None, None))
    return jax.shard_map(local, mesh=fine, in_specs=in_specs, out_specs=out_specs, check_vma=False)
```
